512 devices in a mesh: src: 16 (over y, core), clu: 4 (over x), col: 8 (over z).
Axes of the slice: x: 4, y: 8, z: 8, core: 2. Of those that a mesh axis runs over, the one named last changes fastest.
Arguments:
- embed: bfloat16 [163840, 1024], P(('src', 'clu', 'col')), may hold values from -6 to 6
- assign: int32 [163840], P(('src', 'clu', 'col')), may hold values from 0 to 575, as said below
- slot: int32 [163840], P(('src', 'clu', 'col')), may hold values from 0 to 1023, as said below
Outputs:
- near_max: float32 [512, 512], P(('src', 'clu', 'col'))
- near_cos: float32 [512, 512], P(('src', 'clu', 'col'))
- centroids: float32 [512, 1024], P(('src', 'clu', 'col'))
- giant_max: float32 [64, 1024], P(('src', 'clu'), 'col')
- giant_cos: float32 [64, 1024], P(('src', 'clu'), 'col')
- giant_centroids: float32 [64, 1024], P(('src', 'clu'))
The draws below stay inside these ranges and needn't reach their ends.
Inputs may be any that keep to these rules, and one draw needn't show every extreme that they name: `assign`: each aligned block of 320 rows is one source b (numbered in the mesh's order, b = h * 8 + q with q its col index). Values below 512 name ordinary clusters, 512 + g names giant cluster g. Every cluster is named. For an ordinary cluster slot = b + k with k < 1; for a giant cluster slot = q * 128 + h * 2 + k with k < 2, where q is the source's col index and h = b // 8. No two rows of one cluster share a slot. In every draw some ordinary cluster has all 512 positions filled and some giant cluster has all 1024 positions filled.
All inputs are finite; a program needn't handle non-finite values.
Results may differ from the reference program's by a relative error of at most 0.0029.
Values may be sent and summed in bfloat16 or wider, within the bound.
No kernel may reach another device: no remote copies, remote signals or barrier semaphores. Data moves between devices by JAX's collectives and lax.ppermute only.
A program may use at most 64 MiB of HBM per device.

```python
import jax
import jax.numpy as jnp
from jax import lax

D = 1024
SC = 1
SG = 2
OWNERS = 512
GIANTS = 64
ROWS_DEV = 320
TOKENS = 163840
BLK = 512
GB = 128
GIANT = 1024
N_COL = 8
DEVICES = 512


def clusters_and_slots(key):
    normal_size = DEVICES * SC
    table = normal_size + GIANTS * SG
    favored = jax.random.randint(jax.random.fold_in(key, 11), (), 0, DEVICES)
    favored_giant = jax.random.randint(jax.random.fold_in(key, 13), (), 0, GIANTS)
    entries = jnp.arange(table, dtype=jnp.int32)
    is_giant = entries >= normal_size
    owner = jnp.where(is_giant, (entries - normal_size) // SG, entries // SC)
    place = jnp.where(is_giant, (entries - normal_size) % SG, entries % SC)
    preferred = jnp.where(is_giant, owner == favored_giant, owner == favored)

    def one_source(source):
        first = jax.random.fold_in(jax.random.fold_in(key, 17), source)
        second = jax.random.fold_in(jax.random.fold_in(key, 23), source)
        order = jax.random.permutation(first, table).astype(jnp.int32)
        score = jnp.where(preferred, order - table, order)
        chosen = jnp.argsort(score, stable=True)[:ROWS_DEV].astype(jnp.int32)
        chosen = chosen[jax.random.permutation(second, ROWS_DEV)]
        target = owner[chosen]
        position = place[chosen]
        giant = is_giant[chosen]
        cluster = jnp.where(giant, DEVICES + target, target)
        where_in = jnp.where(giant, source % N_COL * GB + source // N_COL * SG + position, source * SC + position)
        return (cluster.astype(jnp.int32), where_in.astype(jnp.int32))
    cluster, where_in = jax.vmap(one_source)(jnp.arange(DEVICES, dtype=jnp.int32))
    return (cluster.reshape(-1), where_in.reshape(-1))


def draw_assign(key, part):
    return clusters_and_slots(key)[0]


def draw_slot(key, part):
    return clusters_and_slots(key)[1]


def levels(own_key, dims, split, least, top_value):
    def one(dim, parts):
        heights = jax.random.uniform(jax.random.fold_in(jax.random.fold_in(own_key, 6), dim), (parts,), jnp.float32, least / len(split), top_value / len(split))
        return jnp.repeat(jnp.exp(heights), dims[dim] // parts).reshape((-1,) + (1,) * (len(dims) - dim - 1))

    loudness = one(*split[0])
    for cut in split[1:]:
        loudness = loudness * one(*cut)
    return loudness


def scatter_about(rng, shape, spread, most, split=(), kind=jnp.bfloat16):
    factor_of = levels(rng, shape, split, -0.22, 0.18) if split else 1.0
    drawn = jax.random.normal(rng, shape, jnp.float32) * spread * factor_of
    return jnp.minimum(jnp.maximum(drawn, -most), most).astype(kind)


def setup_inputs(seed: int = 0) -> dict:
    keys = jax.random.split(jax.random.key(seed), 4)
    embed = scatter_about(keys[0], (TOKENS, D), 1.0, 6.0, ((0, 512),))
    assign = draw_assign(jax.random.fold_in(keys[3], 71), 0)
    slot = draw_slot(jax.random.fold_in(keys[3], 71), 0)
    return {"embed": embed, "assign": assign, "slot": slot}


EPS = 1e-06

def unit_rows(embed):
    values = embed.astype(jnp.float32)
    return (values * lax.rsqrt(lax.optimization_barrier(jnp.sum(values * values, axis=1, keepdims=True)) + EPS)).astype(jnp.bfloat16)

def occupied(rows):
    values = rows.astype(jnp.float32)
    return lax.optimization_barrier(jnp.sum(values * values, axis=1)) > 0.25

def pair_sims(left, right):
    return lax.dot_general(left, right, (((1,), (1,)), ((), ())), preferred_element_type=jnp.float32)

def normalized(total):
    return total * lax.rsqrt(jnp.sum(total * total) + EPS)

def cosines(rows, live, center):
    return jnp.where(live, lax.optimization_barrier(jnp.sum(rows.astype(jnp.float32) * center[None, :], axis=1)), 0.0)

def block_stats(rows):
    live = occupied(rows)
    sims = pair_sims(rows, rows)
    index = jnp.arange(rows.shape[0], dtype=jnp.int32)
    keep = live[None, :] & (index[:, None] != index[None, :])
    best = lax.optimization_barrier(jnp.max(jnp.where(keep, sims, -4.0), axis=1))
    best = jnp.where(live, best, 0.0)
    total = lax.optimization_barrier(jnp.sum(jnp.where(live[:, None], rows.astype(jnp.float32), 0.0), axis=0))
    center = normalized(total)
    return (best, cosines(rows, live, center), center)

def reference(embed, assign, slot):
    unit = unit_rows(embed)
    giant = assign >= OWNERS
    place = jnp.where(giant, OWNERS * BLK, assign * BLK + slot).astype(jnp.int32)
    normal = jnp.zeros((OWNERS * BLK, D), jnp.bfloat16).at[place].set(unit, mode='drop').reshape(OWNERS, BLK, D)
    gplace = jnp.where(giant, (assign - OWNERS) * GIANT + slot, GIANTS * GIANT).astype(jnp.int32)
    giants = jnp.zeros((GIANTS * GIANT, D), jnp.bfloat16).at[gplace].set(unit, mode='drop').reshape(GIANTS, GIANT, D)
    near_max, near_cos, centroids = lax.map(block_stats, normal)
    giant_max, giant_cos, giant_centroids = lax.map(block_stats, giants)
    return (near_max, near_cos, centroids, giant_max, giant_cos, giant_centroids)
```

```python
import jax
import jax.numpy as jnp
from jax import lax
from jax.experimental import pallas as pl
from jax.experimental.pallas import tpu as pltpu
from jax.sharding import Mesh
from jax.sharding import PartitionSpec as P

N_COL = 8
N_SRC = 16
GROUP = 64
OWNERS = GROUP * N_COL
CHIPS = OWNERS // 2
RUN = 32
WIDTH = 1024
LANES = 128
SUB = WIDTH // LANES
EPS = 1e-06
NONE = -4.0

BF = jnp.bfloat16
F32 = jnp.float32


LONG = pl.CostEstimate(flops=30_000_000_000, bytes_accessed=2_000_000, transcendentals=0)


def params(mib=12):
    return pltpu.CompilerParams(vmem_limit_bytes=mib * 1024 * 1024)


def dot_t(left, right):
    return lax.dot_general(left, right, (((1,), (1,)), ((), ())), preferred_element_type=F32)


def dot(left, right):
    return jnp.dot(left, right, preferred_element_type=F32)


def three(values):
    high = values.astype(BF)
    rest = values - high.astype(F32)
    mid = rest.astype(BF)
    low = (rest - mid.astype(F32)).astype(BF)
    return high, mid, low


def sign_and_col():
    return 1 - 2 * lax.axis_index("core"), lax.axis_index("col")


def placed(rows, target, start, count):
    places = lax.broadcasted_iota(jnp.int32, (count, target.shape[1]), 0) + start
    pick = jnp.where(places == target, 1.0, 0.0).astype(BF)
    return dot(pick, rows).astype(BF)


def giant_pack_kernel(embed_hbm, assign_ref, slot_ref, giant_ref, unit_ref, lines_ref, embed_ref, sem):
    copy = pltpu.make_async_copy(embed_hbm, embed_ref, sem)
    copy.start()
    assign = assign_ref[...].reshape(1, -1)
    lines_ref[...] = assign
    target = (slot_ref[...].reshape(1, -1) & 1) * GROUP + assign - OWNERS
    target = jnp.where(assign >= OWNERS, target, -1)
    copy.wait()
    values = embed_ref[...].astype(F32)
    unit = (values * lax.rsqrt(jnp.sum(values * values, axis=1, keepdims=True) + EPS)).astype(BF)
    unit_ref[...] = unit
    for number in range(2):
        rows = placed(unit, target, number * GROUP, GROUP)
        giant_ref[:, number] = rows.reshape(GROUP, SUB, LANES)


def giant_pack(embed, assign, slot):
    vmem = pl.BlockSpec(memory_space=pltpu.VMEM)
    return pl.pallas_call(
        giant_pack_kernel,
        in_specs=[pl.BlockSpec(memory_space=pl.ANY), vmem, vmem],
        out_shape=[
            jax.ShapeDtypeStruct((GROUP, 2, SUB, LANES), BF),
            jax.ShapeDtypeStruct(embed.shape, BF),
            jax.ShapeDtypeStruct((1, assign.shape[0]), jnp.int32),
        ],
        scratch_shapes=[pltpu.VMEM(embed.shape, BF), pltpu.SemaphoreType.DMA],
        compiler_params=params(56),
        name="giant_pack",
    )(embed, assign, slot)


def pack_kernel(unit_ref, assign_ref, same_ref, other_ref):
    core = lax.axis_index("core")
    assign = assign_ref[...]
    chip = (assign // (2 * RUN)) * RUN + (assign & (RUN - 1))
    other = ((assign // RUN) & 1) != core
    target = jnp.where(assign >= OWNERS, -1, jnp.where(other, CHIPS, 0) + chip)
    unit = unit_ref[...]
    for start in range(0, CHIPS, GROUP):
        rows = placed(unit, target, CHIPS + start, GROUP)
        other_ref[start : start + GROUP] = rows.reshape(GROUP, SUB, LANES)
        rows = placed(unit, target, start, GROUP)
        same_ref[start : start + GROUP] = rows.reshape(GROUP, SUB, LANES)


def pack(unit, assign):
    return pl.pallas_call(
        pack_kernel,
        out_shape=[jax.ShapeDtypeStruct((CHIPS, SUB, LANES), BF)] * 2,
        compiler_params=params(),
        name="pack",
    )(unit, assign)


def join_kernel(same_ref, other_ref, both_ref):
    core = lax.axis_index("core")
    both_ref[:, pl.ds(core, 1)] = same_ref[...].reshape(CHIPS, 1, SUB, LANES)
    both_ref[:, pl.ds(1 - core, 1)] = other_ref[...].reshape(CHIPS, 1, SUB, LANES)


def join(same, other):
    return pl.pallas_call(
        join_kernel,
        out_shape=jax.ShapeDtypeStruct((CHIPS, 2, SUB, LANES), BF),
        compiler_params=params(),
        name="join",
    )(same, other)


def matrix_kernel(tiles_ref, rows_ref):
    rows_ref[...] = tiles_ref[...].reshape(2 * GROUP, WIDTH)


def matrix(tiles):
    return pl.pallas_call(
        matrix_kernel,
        out_shape=jax.ShapeDtypeStruct((2 * GROUP, WIDTH), BF),
        compiler_params=params(),
        name="matrix",
    )(tiles)


def eye(size):
    return lax.broadcasted_iota(jnp.int32, (size, size), 0) == lax.broadcasted_iota(
        jnp.int32, (size, size), 1
    )


def live_of(rows):
    squares = dot_t(rows, rows)
    diagonal = jnp.where(eye(rows.shape[0]), squares, NONE)
    down = jnp.max(diagonal, axis=1, keepdims=True) > 0.25
    across = jnp.max(diagonal, axis=0, keepdims=True) > 0.25
    return squares, down, across


def top(sims, down):
    return jnp.max(jnp.where(down, sims, NONE), axis=0, keepdims=True)


def block_sum(rows, across):
    mask = jnp.broadcast_to(jnp.where(across, 1.0, 0.0), (8, rows.shape[0])).astype(BF)
    return dot(mask, rows)[0:1]


def pairs_kernel(mine_ref, near_ref, far_ref, back_ref, best_ref, sums_ref, one_ref, two_ref):
    size = 2 * GROUP
    mine, near, far, back = mine_ref[...], near_ref[...], far_ref[...], back_ref[...]
    squares, mine_down, mine_across = live_of(mine)
    _, near_down, near_across = live_of(near)
    _, far_down, far_across = live_of(far)
    _, back_down, back_across = live_of(back)
    best = top(squares, mine_down & ~eye(size))
    best = jnp.maximum(best, top(dot_t(near, mine), near_down))
    best = jnp.maximum(best, top(dot_t(far, mine), far_down))
    best_ref[...] = jnp.maximum(best, top(dot_t(back, mine), back_down))
    best_near = jnp.maximum(top(dot_t(mine, near), mine_down), top(dot_t(far, near), far_down))
    best_far = jnp.maximum(top(dot_t(near, far), near_down), top(dot_t(back, far), back_down))
    sum_mine = block_sum(mine, mine_across)
    sum_near = block_sum(near, near_across)
    sum_far = block_sum(far, far_across)
    sum_back = block_sum(back, back_across)
    sums_ref[0:1] = sum_mine
    sums_ref[1:2] = sum_near
    sums_ref[2:3] = sum_far
    sums_ref[3:4] = sum_back
    one_ref[0:1] = sum_mine
    one_ref[1:2] = sum_far
    one_ref[2:3] = jnp.concatenate([best_near] * SUB, axis=1)
    two_ref[0:1] = sum_near
    two_ref[1:2] = sum_back
    two_ref[2:3] = jnp.concatenate([best_far] * SUB, axis=1)


def pairs(mine, near, far, back):
    message = jax.ShapeDtypeStruct((3, WIDTH), F32)
    return pl.pallas_call(
        pairs_kernel,
        out_shape=[
            jax.ShapeDtypeStruct((1, 2 * GROUP), F32),
            jax.ShapeDtypeStruct((4, WIDTH), F32),
            message,
            message,
        ],
        compiler_params=params(),
        cost_estimate=LONG,
        name="pairs",
    )(mine, near, far, back)


def normalized(total):
    return total * lax.rsqrt(jnp.sum(total * total) + EPS)


def cosines(center, rows):
    high, mid, low = three(center)
    parts = jnp.concatenate([high, mid, low, jnp.zeros((5, WIDTH), BF)], axis=0)
    found = dot_t(parts, rows)
    return found[0:1] + found[1:2] + found[2:3]


def giant_kernel(mine_ref, best_ref, sums_ref, one_ref, two_ref, max_ref, cos_ref, center_ref, held):
    sign, col = sign_and_col()
    mine = mine_ref[...]
    _, _, across = live_of(mine)
    best = best_ref[...]
    for ref in (one_ref, two_ref):
        best = jnp.maximum(best, ref[2:3, : 2 * GROUP])
    max_ref[...] = jnp.where(across, best, 0.0)
    for offset, row in (
        (0, sums_ref[0:1]),
        (1, sums_ref[1:2]),
        (6, sums_ref[2:3]),
        (2, sums_ref[3:4]),
        (7, one_ref[0:1]),
        (5, one_ref[1:2]),
        (3, two_ref[0:1]),
        (4, two_ref[1:2]),
    ):
        held[pl.ds((col + sign * offset) & (N_COL - 1), 1)] = row
    total = held[0:1]
    for number in range(1, N_COL):
        total = total + held[number : number + 1]
    center = normalized(total)
    center_ref[...] = center
    cos_ref[...] = jnp.where(across, cosines(center, mine), 0.0)


def giant_stats(*operands):
    return pl.pallas_call(
        giant_kernel,
        out_shape=[
            jax.ShapeDtypeStruct((1, 2 * GROUP), F32),
            jax.ShapeDtypeStruct((1, 2 * GROUP), F32),
            jax.ShapeDtypeStruct((1, WIDTH), F32),
        ],
        scratch_shapes=[pltpu.VMEM((N_COL, WIDTH), F32)],
        compiler_params=params(),
        name="giants",
    )(*operands)


def normal_kernel(tiles_ref, max_ref, cos_ref, center_ref, rows_ref):
    for y in range(CHIPS // RUN):
        for core in range(2):
            start = (2 * y + core) * RUN
            rows_ref[start : start + RUN] = tiles_ref[y * RUN : (y + 1) * RUN, core].reshape(
                RUN, WIDTH
            )
    rows = rows_ref[...]
    squares, down, across = live_of(rows)
    max_ref[...] = jnp.where(across, top(squares, down & ~eye(OWNERS)), 0.0)
    center = normalized(block_sum(rows, across))
    center_ref[...] = center
    cos_ref[...] = jnp.where(across, cosines(center, rows), 0.0)


def normal_stats(tiles):
    return pl.pallas_call(
        normal_kernel,
        out_shape=[
            jax.ShapeDtypeStruct((1, OWNERS), F32),
            jax.ShapeDtypeStruct((1, OWNERS), F32),
            jax.ShapeDtypeStruct((1, WIDTH), F32),
        ],
        scratch_shapes=[pltpu.VMEM((OWNERS, WIDTH), BF)],
        compiler_params=params(),
        name="ordinary",
    )(tiles)


def along(rows, offset):
    moves = []
    for src in range(N_SRC):
        for col in range(N_COL):
            goal = (col + (offset if src % 2 == 0 else -offset)) % N_COL
            moves.append((src * N_COL + col, src * N_COL + goal))
    return lax.ppermute(rows, ("y", "core", "col"), moves)


def to_other_core(rows):
    return lax.ppermute(rows, "core", [(0, 1), (1, 0)])


def all_to_all(rows, axes):
    return lax.all_to_all(rows, axes, split_axis=0, concat_axis=0, tiled=True)


def per_device(embed, assign, slot):
    giant, unit, lines = giant_pack(embed, assign, slot)
    giant = all_to_all(giant, ("y", "core", "clu"))
    same, other = pack(unit, lines)
    both = join(same, to_other_core(other))
    mine = matrix(giant)
    near, far, back = along(mine, 7), along(mine, 2), along(mine, 6)
    both = all_to_all(both, ("y", "clu", "col"))
    best, sums, one, two = pairs(mine, near, far, back)
    one, two = along(one, 1), along(two, 6)
    giant_max, giant_cos, giant_center = giant_stats(mine, best, sums, one, two)
    near_max, near_cos, center = normal_stats(both)
    return near_max, near_cos, center, giant_max, giant_cos, giant_center


def solution(mesh):
    fine = Mesh(mesh.devices.reshape(N_SRC // 2, 2, -1, N_COL), ("y", "core", "clu", "col"))
    plane = ("y", "core", "clu")
    everywhere = (*plane, "col")
    in_specs = (P(everywhere, None), P(everywhere), P(everywhere))
    out_specs = (
        P(everywhere, None),
        P(everywhere, None),
        P(everywhere, None),
        P(plane, "col"),
        P(plane, "col"),
        P(plane, None),
    )
    return jax.shard_map(
        per_device, mesh=fine, in_specs=in_specs, out_specs=out_specs, check_vma=False
    )
```

```python
import jax
import jax.numpy as jnp
from jax import lax
from jax.experimental import pallas as pl
from jax.experimental.pallas import tpu as pltpu
from jax.sharding import Mesh
from jax.sharding import PartitionSpec as P

N_COL = 8
N_SRC = 16
GROUP = 64
OWNERS = GROUP * N_COL
CHIPS = OWNERS // 2
RUN = 32
WIDTH = 1024
LANES = 128
SUB = WIDTH // LANES
EPS = 1e-06
NONE = -4.0

BF = jnp.bfloat16
F32 = jnp.float32


LONG = pl.CostEstimate(flops=30_000_000_000, bytes_accessed=2_000_000, transcendentals=0)


def params(mib=12):
    return pltpu.CompilerParams(vmem_limit_bytes=mib * 1024 * 1024)


def dot_t(left, right):
    return lax.dot_general(left, right, (((1,), (1,)), ((), ())), preferred_element_type=F32)


def dot(left, right):
    return jnp.dot(left, right, preferred_element_type=F32)


def three(values):
    high = values.astype(BF)
    rest = values - high.astype(F32)
    mid = rest.astype(BF)
    low = (rest - mid.astype(F32)).astype(BF)
    return high, mid, low


def sign_and_col():
    return 1 - 2 * lax.axis_index("core"), lax.axis_index("col")


def unit_rows(rows):
    values = rows.astype(F32)
    return (values * lax.rsqrt(jnp.sum(values * values, axis=1, keepdims=True) + EPS)).astype(BF)


def placed(rows, target, start, count):
    places = lax.broadcasted_iota(jnp.int32, (count, target.shape[1]), 0) + start
    pick = jnp.where(places == target, 1.0, 0.0).astype(BF)
    return dot(pick, rows).astype(BF)


def giant_pack_kernel(
    embed_hbm, assign_hbm, slot_hbm, giant_ref, lines_ref, embed_ref, assign_ref, slot_ref, sems
):
    parts = (pl.ds(0, LANES), pl.ds(LANES, embed_ref.shape[0] - LANES))
    copies = [
        pltpu.make_async_copy(assign_hbm, assign_ref, sems.at[0]),
        pltpu.make_async_copy(slot_hbm, slot_ref, sems.at[1]),
    ]
    copies += [
        pltpu.make_async_copy(embed_hbm.at[part], embed_ref.at[part], sems.at[2 + number])
        for number, part in enumerate(parts)
    ]
    for copy in copies:
        copy.start()
    copies[0].wait()
    copies[1].wait()
    assign = assign_ref[...].reshape(1, -1)
    lines_ref[...] = assign
    target = (slot_ref[...].reshape(1, -1) & 1) * GROUP + assign - OWNERS
    target = jnp.where(assign >= OWNERS, target, -1)
    places = lax.broadcasted_iota(jnp.int32, (2 * GROUP, target.shape[1]), 0)
    pick = jnp.where(places == target, 1.0, 0.0).astype(BF)
    copies[2].wait()
    rows = dot(pick[:, :LANES], unit_rows(embed_ref[:LANES]))
    copies[3].wait()
    rows = (rows + dot(pick[:, LANES:], unit_rows(embed_ref[LANES:]))).astype(BF)
    for number in range(2):
        part = rows[number * GROUP : (number + 1) * GROUP]
        giant_ref[:, number] = part.reshape(GROUP, SUB, LANES)


def giant_pack(embed, assign, slot):
    return pl.pallas_call(
        giant_pack_kernel,
        in_specs=[pl.BlockSpec(memory_space=pl.ANY)] * 3,
        out_shape=[
            jax.ShapeDtypeStruct((GROUP, 2, SUB, LANES), BF),
            jax.ShapeDtypeStruct((1, assign.shape[0]), jnp.int32),
        ],
        scratch_shapes=[
            pltpu.VMEM(embed.shape, BF),
            pltpu.VMEM(assign.shape, jnp.int32),
            pltpu.VMEM(slot.shape, jnp.int32),
            pltpu.SemaphoreType.DMA((4,)),
        ],
        compiler_params=params(56),
        name="giant_pack",
    )(embed, assign, slot)


def pack_kernel(embed_ref, assign_ref, same_ref, other_ref):
    core = lax.axis_index("core")
    assign = assign_ref[...]
    chip = (assign // (2 * RUN)) * RUN + (assign & (RUN - 1))
    other = ((assign // RUN) & 1) != core
    target = jnp.where(assign >= OWNERS, -1, jnp.where(other, CHIPS, 0) + chip)
    unit = unit_rows(embed_ref[...])
    for start in range(0, CHIPS, GROUP):
        rows = placed(unit, target, CHIPS + start, GROUP)
        other_ref[start : start + GROUP] = rows.reshape(GROUP, SUB, LANES)
        rows = placed(unit, target, start, GROUP)
        same_ref[start : start + GROUP] = rows.reshape(GROUP, SUB, LANES)


def pack(embed, assign):
    return pl.pallas_call(
        pack_kernel,
        out_shape=[jax.ShapeDtypeStruct((CHIPS, SUB, LANES), BF)] * 2,
        compiler_params=params(),
        name="pack",
    )(embed, assign)


def join_kernel(same_ref, other_ref, both_ref, sems):
    core = lax.axis_index("core")
    copies = [
        pltpu.make_async_copy(same_ref, both_ref.at[:, core], sems.at[0]),
        pltpu.make_async_copy(other_ref, both_ref.at[:, 1 - core], sems.at[1]),
    ]
    for copy in copies:
        copy.start()
    for copy in copies:
        copy.wait()


def join(same, other):
    return pl.pallas_call(
        join_kernel,
        in_specs=[pl.BlockSpec(memory_space=pl.ANY)] * 2,
        out_specs=pl.BlockSpec(memory_space=pl.ANY),
        out_shape=jax.ShapeDtypeStruct((CHIPS, 2, SUB, LANES), BF),
        scratch_shapes=[pltpu.SemaphoreType.DMA((2,))],
        compiler_params=params(),
        name="join",
    )(same, other)


def block(ref):
    return ref[...].reshape(2 * GROUP, WIDTH)


def eye(size):
    return lax.broadcasted_iota(jnp.int32, (size, size), 0) == lax.broadcasted_iota(
        jnp.int32, (size, size), 1
    )


def live_of(rows):
    squares = dot_t(rows, rows)
    diagonal = jnp.where(eye(rows.shape[0]), squares, NONE)
    down = jnp.max(diagonal, axis=1, keepdims=True) > 0.25
    across = jnp.max(diagonal, axis=0, keepdims=True) > 0.25
    return squares, down, across


def top(sims, down):
    return jnp.max(jnp.where(down, sims, NONE), axis=0, keepdims=True)


def block_sum(rows, across):
    mask = jnp.broadcast_to(jnp.where(across, 1.0, 0.0), (8, rows.shape[0])).astype(BF)
    return dot(mask, rows)[0:1]


def pairs_kernel(mine_ref, near_ref, far_ref, best_ref, sums_ref, one_ref, two_ref):
    size = 2 * GROUP
    mine, near, far = block(mine_ref), block(near_ref), block(far_ref)
    squares, mine_down, mine_across = live_of(mine)
    _, near_down, near_across = live_of(near)
    _, far_down, far_across = live_of(far)
    best = top(squares, mine_down & ~eye(size))
    best = jnp.maximum(best, top(dot_t(near, mine), near_down))
    best_ref[...] = jnp.maximum(best, top(dot_t(far, mine), far_down))
    best_near = jnp.maximum(top(dot_t(mine, near), mine_down), top(dot_t(far, near), far_down))
    best_far = jnp.maximum(top(dot_t(mine, far), mine_down), top(dot_t(near, far), near_down))
    sum_mine = block_sum(mine, mine_across)
    sum_near = block_sum(near, near_across)
    sum_far = block_sum(far, far_across)
    sums_ref[0:1] = sum_mine
    sums_ref[1:2] = sum_near
    sums_ref[2:3] = sum_far
    one_ref[0:1] = sum_mine
    one_ref[1:2] = sum_far
    one_ref[2:3] = jnp.concatenate([best_near] * SUB, axis=1)
    two_ref[0:1] = sum_mine
    two_ref[1:2] = sum_near
    two_ref[2:3] = jnp.concatenate([best_far] * SUB, axis=1)


def pairs(mine, near, far):
    message = jax.ShapeDtypeStruct((3, WIDTH), F32)
    return pl.pallas_call(
        pairs_kernel,
        out_shape=[jax.ShapeDtypeStruct((1, 2 * GROUP), F32), message, message, message],
        compiler_params=params(),
        cost_estimate=LONG,
        name="pairs",
    )(mine, near, far)


def normalized(total):
    return total * lax.rsqrt(jnp.sum(total * total) + EPS)


def cosines(center, rows):
    high, mid, low = three(center)
    parts = jnp.concatenate([high, mid, low, jnp.zeros((5, WIDTH), BF)], axis=0)
    found = dot_t(parts, rows)
    return found[0:1] + found[1:2] + found[2:3]


def giant_kernel(
    _, mine_ref, last_ref, best_ref, sums_ref, one_ref, two_ref, max_ref, cos_ref, center_ref, held
):
    sign, col = sign_and_col()
    mine, last = block(mine_ref), block(last_ref)
    _, _, across = live_of(mine)
    _, last_down, last_across = live_of(last)
    best = jnp.maximum(best_ref[...], top(dot_t(last, mine), last_down))
    for ref in (one_ref, two_ref):
        best = jnp.maximum(best, ref[2:3, : 2 * GROUP])
    max_ref[...] = jnp.where(across, best, 0.0)
    for offset, row in (
        (0, sums_ref[0:1]),
        (1, sums_ref[1:2]),
        (3, sums_ref[2:3]),
        (4, block_sum(last, last_across)),
        (7, one_ref[0:1]),
        (2, one_ref[1:2]),
        (5, two_ref[0:1]),
        (6, two_ref[1:2]),
    ):
        held[pl.ds((col + sign * offset) & (N_COL - 1), 1)] = row
    total = held[0:1]
    for number in range(1, N_COL):
        total = total + held[number : number + 1]
    center = normalized(total)
    center_ref[...] = center
    cos_ref[...] = jnp.where(across, cosines(center, mine), 0.0)


def giant_stats(ready, *operands):
    vmem = pl.BlockSpec(memory_space=pltpu.VMEM)
    return pl.pallas_call(
        giant_kernel,
        in_specs=[pl.BlockSpec(memory_space=pl.ANY)] + [vmem] * len(operands),
        out_shape=[
            jax.ShapeDtypeStruct((1, 2 * GROUP), F32),
            jax.ShapeDtypeStruct((1, 2 * GROUP), F32),
            jax.ShapeDtypeStruct((1, WIDTH), F32),
        ],
        scratch_shapes=[pltpu.VMEM((N_COL, WIDTH), F32)],
        compiler_params=params(),
        name="giants",
    )(ready, *operands)


def normal_kernel(tiles_ref, max_ref, cos_ref, center_ref, done_ref, rows_ref):
    for y in range(CHIPS // RUN):
        for core in range(2):
            start = (2 * y + core) * RUN
            rows_ref[start : start + RUN] = tiles_ref[y * RUN : (y + 1) * RUN, core].reshape(
                RUN, WIDTH
            )
    done_ref[...] = jnp.zeros_like(done_ref)
    rows = rows_ref[...]
    squares, down, across = live_of(rows)
    max_ref[...] = jnp.where(across, top(squares, down & ~eye(OWNERS)), 0.0)
    center = normalized(block_sum(rows, across))
    center_ref[...] = center
    cos_ref[...] = jnp.where(across, cosines(center, rows), 0.0)


def normal_stats(tiles):
    return pl.pallas_call(
        normal_kernel,
        out_shape=[
            jax.ShapeDtypeStruct((1, OWNERS), F32),
            jax.ShapeDtypeStruct((1, OWNERS), F32),
            jax.ShapeDtypeStruct((1, WIDTH), F32),
            jax.ShapeDtypeStruct((8, LANES), F32),
        ],
        scratch_shapes=[pltpu.VMEM((OWNERS, WIDTH), BF)],
        compiler_params=params(),
        name="ordinary",
    )(tiles)


def along(rows, offset):
    moves = []
    for src in range(N_SRC):
        for col in range(N_COL):
            goal = (col + (offset if src % 2 == 0 else -offset)) % N_COL
            moves.append((src * N_COL + col, src * N_COL + goal))
    return lax.ppermute(rows, ("y", "core", "col"), moves)


def to_other_core(rows):
    return lax.ppermute(rows, "core", [(0, 1), (1, 0)])


def all_to_all(rows, axes):
    return lax.all_to_all(rows, axes, split_axis=0, concat_axis=0, tiled=True)


def per_device(embed, assign, slot):
    giant, lines = giant_pack(embed, assign, slot)
    giant = all_to_all(giant, ("y", "core", "clu"))
    same, other = pack(embed, lines)
    both = join(same, to_other_core(other))
    mine = giant
    near, far = along(mine, 7), along(mine, 5)
    both = all_to_all(both, ("y", "clu", "col"))
    last = along(far, 7)
    best, sums, one, two = pairs(mine, near, far)
    one, two = along(one, 1), along(two, 3)
    near_max, near_cos, center, done = normal_stats(both)
    giant_max, giant_cos, giant_center = giant_stats(done, mine, last, best, sums, one, two)
    return near_max, near_cos, center, giant_max, giant_cos, giant_center


def solution(mesh):
    fine = Mesh(mesh.devices.reshape(N_SRC // 2, 2, -1, N_COL), ("y", "core", "clu", "col"))
    plane = ("y", "core", "clu")
    everywhere = (*plane, "col")
    in_specs = (P(everywhere, None), P(everywhere), P(everywhere))
    out_specs = (
        P(everywhere, None),
        P(everywhere, None),
        P(everywhere, None),
        P(plane, "col"),
        P(plane, "col"),
        P(plane, None),
    )
    return jax.shard_map(
        per_device, mesh=fine, in_specs=in_specs, out_specs=out_specs, check_vma=False
    )
```

```python
import jax
import jax.numpy as jnp
from jax import lax
from jax.experimental import pallas as pl
from jax.experimental.pallas import tpu as pltpu
from jax.sharding import Mesh
from jax.sharding import PartitionSpec as P

N_COL = 8
N_SRC = 16
GROUP = 64
OWNERS = GROUP * N_COL
CHIPS = OWNERS // 2
RUN = 32
WIDTH = 1024
LANES = 128
SUB = WIDTH // LANES
EPS = 1e-06
NONE = -4.0

BF = jnp.bfloat16
F32 = jnp.float32


LONG = pl.CostEstimate(flops=30_000_000_000, bytes_accessed=2_000_000, transcendentals=0)


def params(mib=12):
    return pltpu.CompilerParams(vmem_limit_bytes=mib * 1024 * 1024)


def dot_t(left, right):
    return lax.dot_general(left, right, (((1,), (1,)), ((), ())), preferred_element_type=F32)


def dot(left, right):
    return jnp.dot(left, right, preferred_element_type=F32)


def three(values):
    high = values.astype(BF)
    rest = values - high.astype(F32)
    mid = rest.astype(BF)
    low = (rest - mid.astype(F32)).astype(BF)
    return high, mid, low


def sign_and_col():
    return 1 - 2 * lax.axis_index("core"), lax.axis_index("col")


def unit_rows(rows):
    values = rows.astype(F32)
    return (values * lax.rsqrt(jnp.sum(values * values, axis=1, keepdims=True) + EPS)).astype(BF)


def placed(rows, target, start, count):
    places = lax.broadcasted_iota(jnp.int32, (count, target.shape[1]), 0) + start
    pick = jnp.where(places == target, 1.0, 0.0).astype(BF)
    return dot(pick, rows).astype(BF)


def giant_pack_kernel(
    embed_hbm, assign_hbm, slot_hbm, giant_ref, lines_ref, embed_ref, assign_ref, slot_ref, sems
):
    parts = (pl.ds(0, LANES), pl.ds(LANES, embed_ref.shape[0] - LANES))
    copies = [
        pltpu.make_async_copy(assign_hbm, assign_ref, sems.at[0]),
        pltpu.make_async_copy(slot_hbm, slot_ref, sems.at[1]),
    ]
    copies += [
        pltpu.make_async_copy(embed_hbm.at[part], embed_ref.at[part], sems.at[2 + number])
        for number, part in enumerate(parts)
    ]
    for copy in copies:
        copy.start()
    copies[0].wait()
    copies[1].wait()
    assign = assign_ref[...].reshape(1, -1)
    lines_ref[...] = assign
    target = (slot_ref[...].reshape(1, -1) & 1) * GROUP + assign - OWNERS
    target = jnp.where(assign >= OWNERS, target, -1)
    places = lax.broadcasted_iota(jnp.int32, (2 * GROUP, target.shape[1]), 0)
    pick = jnp.where(places == target, 1.0, 0.0).astype(BF)
    copies[2].wait()
    rows = dot(pick[:, :LANES], embed_ref[:LANES])
    copies[3].wait()
    rows = unit_rows(rows + dot(pick[:, LANES:], embed_ref[LANES:]))
    for number in range(2):
        part = rows[number * GROUP : (number + 1) * GROUP]
        giant_ref[:, number] = part.reshape(GROUP, SUB, LANES)


def giant_pack(embed, assign, slot):
    return pl.pallas_call(
        giant_pack_kernel,
        in_specs=[pl.BlockSpec(memory_space=pl.ANY)] * 3,
        out_shape=[
            jax.ShapeDtypeStruct((GROUP, 2, SUB, LANES), BF),
            jax.ShapeDtypeStruct((1, assign.shape[0]), jnp.int32),
        ],
        scratch_shapes=[
            pltpu.VMEM(embed.shape, BF),
            pltpu.VMEM(assign.shape, jnp.int32),
            pltpu.VMEM(slot.shape, jnp.int32),
            pltpu.SemaphoreType.DMA((4,)),
        ],
        compiler_params=params(56),
        name="giant_pack",
    )(embed, assign, slot)


def pack_kernel(embed_ref, assign_ref, same_ref, other_ref):
    core = lax.axis_index("core")
    assign = assign_ref[...]
    chip = (assign // (2 * RUN)) * RUN + (assign & (RUN - 1))
    other = ((assign // RUN) & 1) != core
    target = jnp.where(assign >= OWNERS, -1, jnp.where(other, CHIPS, 0) + chip)
    unit = unit_rows(embed_ref[...])
    for start in range(0, CHIPS, GROUP):
        rows = placed(unit, target, CHIPS + start, GROUP)
        other_ref[start : start + GROUP] = rows.reshape(GROUP, SUB, LANES)
        rows = placed(unit, target, start, GROUP)
        same_ref[start : start + GROUP] = rows.reshape(GROUP, SUB, LANES)


def pack(embed, assign):
    return pl.pallas_call(
        pack_kernel,
        out_shape=[jax.ShapeDtypeStruct((CHIPS, SUB, LANES), BF)] * 2,
        compiler_params=params(),
        name="pack",
    )(embed, assign)


def join_kernel(same_ref, other_ref, both_ref, sems):
    core = lax.axis_index("core")
    copies = [
        pltpu.make_async_copy(same_ref, both_ref.at[:, core], sems.at[0]),
        pltpu.make_async_copy(other_ref, both_ref.at[:, 1 - core], sems.at[1]),
    ]
    for copy in copies:
        copy.start()
    for copy in copies:
        copy.wait()


def join(same, other):
    return pl.pallas_call(
        join_kernel,
        in_specs=[pl.BlockSpec(memory_space=pl.ANY)] * 2,
        out_specs=pl.BlockSpec(memory_space=pl.ANY),
        out_shape=jax.ShapeDtypeStruct((CHIPS, 2, SUB, LANES), BF),
        scratch_shapes=[pltpu.SemaphoreType.DMA((2,))],
        compiler_params=params(),
        name="join",
    )(same, other)


def block(ref):
    return ref[...].reshape(2 * GROUP, WIDTH)


def eye(size):
    return lax.broadcasted_iota(jnp.int32, (size, size), 0) == lax.broadcasted_iota(
        jnp.int32, (size, size), 1
    )


def live_of(rows):
    products = dot_t(rows, rows)
    down, across = [], []
    for start in range(0, rows.shape[0], LANES):
        part = products[start : start + LANES, start : start + LANES]
        diagonal = jnp.where(eye(LANES), part, NONE)
        down.append(jnp.max(diagonal, axis=1, keepdims=True) > 0.25)
        across.append(jnp.max(diagonal, axis=0, keepdims=True) > 0.25)
    return products, down, jnp.concatenate(across, axis=1)


def top(products, down, own=None):
    best = None
    for number, live in enumerate(down):
        part = products[number * LANES : (number + 1) * LANES]
        part = jnp.where(live & ~eye(LANES) if number == own else live, part, NONE)
        part = jnp.max(part, axis=0, keepdims=True)
        best = part if best is None else jnp.maximum(best, part)
    return best


def column_sum(products, down):
    total = None
    for number, live in enumerate(down):
        part = jnp.where(live, products[number * LANES : (number + 1) * LANES], 0.0)
        part = jnp.sum(part, axis=0, keepdims=True)
        total = part if total is None else total + part
    return total


def block_sum(rows, across):
    mask = jnp.broadcast_to(jnp.where(across, 1.0, 0.0), (8, rows.shape[0])).astype(BF)
    return dot(mask, rows)[0:1]


def first_kernel(mine_ref, near_ref, rows_ref):
    rows_ref[0] = block(mine_ref)
    rows_ref[1] = block(near_ref)


def first_two(mine, near):
    return pl.pallas_call(
        first_kernel,
        out_shape=jax.ShapeDtypeStruct((2, 2 * GROUP, WIDTH), BF),
        compiler_params=params(),
        cost_estimate=LONG,
        name="first_two",
    )(mine, near)


def pairs_kernel(rows_ref, far_ref, best_ref, sums_ref, one_ref, two_ref):
    mine, near, far = rows_ref[0], rows_ref[1], block(far_ref)
    squares, mine_down, mine_across = live_of(mine)
    _, near_down, near_across = live_of(near)
    _, far_down, far_across = live_of(far)
    best = top(squares, mine_down, 0)
    best = jnp.maximum(best, top(dot_t(near, mine), near_down))
    best_ref[0:1] = jnp.maximum(best, top(dot_t(far, mine), far_down))
    best_ref[1:2] = jnp.where(mine_across, 1.0, 0.0)
    best_near = jnp.maximum(top(dot_t(mine, near), mine_down), top(dot_t(far, near), far_down))
    best_far = jnp.maximum(top(dot_t(mine, far), mine_down), top(dot_t(near, far), near_down))
    sum_mine = block_sum(mine, mine_across)
    sum_near = block_sum(near, near_across)
    sum_far = block_sum(far, far_across)
    sums_ref[0:1] = sum_mine
    sums_ref[1:2] = sum_near
    sums_ref[2:3] = sum_far
    one_ref[0:1] = sum_mine
    one_ref[1:2] = sum_far
    one_ref[2:3] = jnp.concatenate([best_near] * SUB, axis=1)
    two_ref[0:1] = sum_mine
    two_ref[1:2] = sum_near
    two_ref[2:3] = jnp.concatenate([best_far] * SUB, axis=1)


def pairs(rows, far):
    message = jax.ShapeDtypeStruct((3, WIDTH), F32)
    return pl.pallas_call(
        pairs_kernel,
        out_shape=[jax.ShapeDtypeStruct((2, 2 * GROUP), F32), message, message, message],
        compiler_params=params(),
        cost_estimate=LONG,
        name="pairs",
    )(rows, far)


def scale_of(total):
    return lax.rsqrt(jnp.sum(total * total) + EPS)


def products_with(total, rows):
    high, mid, low = three(total)
    parts = jnp.concatenate([high, mid, low, jnp.zeros((5, WIDTH), BF)], axis=0)
    found = dot_t(parts, rows)
    return found[0:1] + found[1:2] + found[2:3]


def early_kernel(rows_ref, best_ref, sums_ref, one_ref, two_ref, some_ref, held_ref):
    sign, col = sign_and_col()
    best = best_ref[0:1]
    for ref in (one_ref, two_ref):
        best = jnp.maximum(best, ref[2:3, : 2 * GROUP])
    held_ref[...] = jnp.zeros_like(held_ref)
    total = jnp.zeros((1, WIDTH), F32)
    for offset, row in (
        (0, sums_ref[0:1]),
        (1, sums_ref[1:2]),
        (3, sums_ref[2:3]),
        (7, one_ref[0:1]),
        (2, one_ref[1:2]),
        (5, two_ref[0:1]),
        (6, two_ref[1:2]),
    ):
        held_ref[pl.ds((col + sign * offset) & (N_COL - 1), 1)] = row
        total = total + row
    some_ref[0:1] = best
    some_ref[1:2] = products_with(total, rows_ref[0])
    some_ref[2:3] = best_ref[1:2]


def early(*operands):
    return pl.pallas_call(
        early_kernel,
        out_shape=[
            jax.ShapeDtypeStruct((3, 2 * GROUP), F32),
            jax.ShapeDtypeStruct((N_COL, WIDTH), F32),
        ],
        compiler_params=params(),
        name="early",
    )(*operands)


def tail_kernel(tiles_ref, rows_ref, some_ref, held_ref, last_ref, *refs):
    *outs, scratch_ref = refs
    giant_part(rows_ref, some_ref, held_ref, last_ref, *outs[3:])
    normal_part(tiles_ref, *outs[:3], scratch_ref)


def giant_part(rows_ref, some_ref, held_ref, last_ref, max_ref, cos_ref, center_ref):
    sign, col = sign_and_col()
    last = block(last_ref)
    _, down, across = live_of(last)
    products = dot_t(last, rows_ref[0])
    place = (col + sign * 4) & (N_COL - 1)
    held = held_ref[...]
    is_last = lax.broadcasted_iota(jnp.int32, held.shape, 0) == place
    held = jnp.where(is_last, block_sum(last, across), held)
    total = held[0:1]
    for number in range(1, N_COL):
        total = total + held[number : number + 1]
    scale = scale_of(total)
    live = some_ref[2:3] > 0.0
    max_ref[...] = jnp.where(live, jnp.maximum(some_ref[0:1], top(products, down)), 0.0)
    cos_ref[...] = jnp.where(live, (some_ref[1:2] + column_sum(products, down)) * scale, 0.0)
    center_ref[...] = total * scale


def normal_part(tiles_ref, max_ref, cos_ref, center_ref, rows_ref):
    for y in range(CHIPS // RUN):
        for core in range(2):
            start = (2 * y + core) * RUN
            rows_ref[start : start + RUN] = tiles_ref[y * RUN : (y + 1) * RUN, core].reshape(
                RUN, WIDTH
            )
    rows = rows_ref[...]
    products, down, across = live_of(rows)
    total = block_sum(rows, across)
    scale = scale_of(total)
    center_ref[...] = total * scale
    best = [
        top(products[:, number * LANES : (number + 1) * LANES], down, number)
        for number in range(len(down))
    ]
    max_ref[...] = jnp.where(across, jnp.concatenate(best, axis=1), 0.0)
    cos_ref[...] = jnp.where(across, column_sum(products, down) * scale, 0.0)


def tail(*operands):
    row = lambda size: jax.ShapeDtypeStruct((1, size), F32)
    return pl.pallas_call(
        tail_kernel,
        out_shape=[row(OWNERS), row(OWNERS), row(WIDTH), row(2 * GROUP), row(2 * GROUP), row(WIDTH)],
        scratch_shapes=[pltpu.VMEM((OWNERS, WIDTH), BF)],
        compiler_params=params(),
        name="tail",
    )(*operands)


def along(rows, offset):
    moves = []
    for src in range(N_SRC):
        for col in range(N_COL):
            goal = (col + (offset if src % 2 == 0 else -offset)) % N_COL
            moves.append((src * N_COL + col, src * N_COL + goal))
    return lax.ppermute(rows, ("y", "core", "col"), moves)


def to_other_core(rows):
    return lax.ppermute(rows, "core", [(0, 1), (1, 0)])


def all_to_all(rows, axes):
    return lax.all_to_all(rows, axes, split_axis=0, concat_axis=0, tiled=True)


def per_device(embed, assign, slot):
    giant, lines = giant_pack(embed, assign, slot)
    giant = all_to_all(giant, ("y", "core", "clu"))
    same, other = pack(embed, lines)
    both = join(same, to_other_core(other))
    mine = giant
    near, far = along(mine, 7), along(mine, 5)
    both = all_to_all(both, ("y", "clu", "col"))
    last = along(far, 7)
    rows = first_two(mine, near)
    best, sums, one, two = pairs(rows, far)
    one, two = along(one, 1), along(two, 3)
    some, held = early(rows, best, sums, one, two)
    return tuple(tail(both, rows, some, held, last))


def solution(mesh):
    fine = Mesh(mesh.devices.reshape(N_SRC // 2, 2, -1, N_COL), ("y", "core", "clu", "col"))
    plane = ("y", "core", "clu")
    everywhere = (*plane, "col")
    in_specs = (P(everywhere, None), P(everywhere), P(everywhere))
    out_specs = (
        P(everywhere, None),
        P(everywhere, None),
        P(everywhere, None),
        P(plane, "col"),
        P(plane, "col"),
        P(plane, None),
    )
    return jax.shard_map(
        per_device, mesh=fine, in_specs=in_specs, out_specs=out_specs, check_vma=False
    )
```

```python
import jax
import jax.numpy as jnp
from jax import lax
from jax.experimental import pallas as pl
from jax.experimental.pallas import tpu as pltpu
from jax.sharding import Mesh
from jax.sharding import PartitionSpec as P

N_COL = 8
N_SRC = 16
GROUP = 64
OWNERS = GROUP * N_COL
CHIPS = OWNERS // 2
RUN = 32
WIDTH = 1024
LANES = 128
SUB = WIDTH // LANES
EPS = 1e-06
NONE = -4.0

BF = jnp.bfloat16
F32 = jnp.float32


LONG = pl.CostEstimate(flops=30_000_000_000, bytes_accessed=2_000_000, transcendentals=0)


def params(mib=12):
    return pltpu.CompilerParams(vmem_limit_bytes=mib * 1024 * 1024)


def dot_t(left, right):
    return lax.dot_general(left, right, (((1,), (1,)), ((), ())), preferred_element_type=F32)


def dot(left, right):
    return jnp.dot(left, right, preferred_element_type=F32)


def three(values):
    high = values.astype(BF)
    rest = values - high.astype(F32)
    mid = rest.astype(BF)
    low = (rest - mid.astype(F32)).astype(BF)
    return high, mid, low


def sign_and_col():
    return 1 - 2 * lax.axis_index("core"), lax.axis_index("col")


def unit_rows(rows):
    values = rows.astype(F32)
    return (values * lax.rsqrt(jnp.sum(values * values, axis=1, keepdims=True) + EPS)).astype(BF)


def placed(rows, target, start, count):
    places = lax.broadcasted_iota(jnp.int32, (count, target.shape[1]), 0) + start
    pick = jnp.where(places == target, 1.0, 0.0).astype(BF)
    return dot(pick, rows).astype(BF)


def giant_pack_kernel(
    embed_hbm, assign_hbm, slot_hbm, giant_ref, lines_ref, embed_ref, assign_ref, slot_ref, sems
):
    parts = (pl.ds(0, LANES), pl.ds(LANES, embed_ref.shape[0] - LANES))
    copies = [
        pltpu.make_async_copy(assign_hbm, assign_ref, sems.at[0]),
        pltpu.make_async_copy(slot_hbm, slot_ref, sems.at[1]),
    ]
    copies += [
        pltpu.make_async_copy(embed_hbm.at[part], embed_ref.at[part], sems.at[2 + number])
        for number, part in enumerate(parts)
    ]
    for copy in copies:
        copy.start()
    copies[0].wait()
    copies[1].wait()
    assign = assign_ref[...].reshape(1, -1)
    lines_ref[...] = assign
    target = (slot_ref[...].reshape(1, -1) & 1) * GROUP + assign - OWNERS
    target = jnp.where(assign >= OWNERS, target, -1)
    places = lax.broadcasted_iota(jnp.int32, (2 * GROUP, target.shape[1]), 0)
    pick = jnp.where(places == target, 1.0, 0.0).astype(BF)
    copies[2].wait()
    rows = dot(pick[:, :LANES], embed_ref[:LANES])
    copies[3].wait()
    rows = unit_rows(rows + dot(pick[:, LANES:], embed_ref[LANES:]))
    for number in range(2):
        part = rows[number * GROUP : (number + 1) * GROUP]
        giant_ref[:, number] = part.reshape(GROUP, SUB, LANES)


def giant_pack(embed, assign, slot):
    return pl.pallas_call(
        giant_pack_kernel,
        in_specs=[pl.BlockSpec(memory_space=pl.ANY)] * 3,
        out_shape=[
            jax.ShapeDtypeStruct((GROUP, 2, SUB, LANES), BF),
            jax.ShapeDtypeStruct((1, assign.shape[0]), jnp.int32),
        ],
        scratch_shapes=[
            pltpu.VMEM(embed.shape, BF),
            pltpu.VMEM(assign.shape, jnp.int32),
            pltpu.VMEM(slot.shape, jnp.int32),
            pltpu.SemaphoreType.DMA((4,)),
        ],
        compiler_params=params(56),
        name="giant_pack",
    )(embed, assign, slot)


def pack_kernel(embed_ref, assign_ref, same_ref, *other_refs):
    core = lax.axis_index("core")
    assign = assign_ref[...]
    chip = (assign // (2 * RUN)) * RUN + (assign & (RUN - 1))
    other = ((assign // RUN) & 1) != core
    target = jnp.where(assign >= OWNERS, -1, jnp.where(other, CHIPS, 0) + chip)
    unit = unit_rows(embed_ref[...])
    half = CHIPS // 2
    for number, ref in enumerate(other_refs):
        rows = placed(unit, target, CHIPS + number * half, half)
        ref[...] = rows.reshape(half, SUB, LANES)
    for start in (0, half):
        rows = placed(unit, target, start, half)
        same_ref[start : start + half] = rows.reshape(half, SUB, LANES)


def pack(embed, assign):
    shape = lambda rows: jax.ShapeDtypeStruct((rows, SUB, LANES), BF)
    return pl.pallas_call(
        pack_kernel,
        out_shape=[shape(CHIPS), shape(CHIPS // 2), shape(CHIPS // 2)],
        compiler_params=params(),
        name="pack",
    )(embed, assign)


def join_kernel(same_ref, low_ref, high_ref, both_ref, sems):
    core = lax.axis_index("core")
    half = CHIPS // 2
    copies = [
        pltpu.make_async_copy(same_ref, both_ref.at[:, core], sems.at[0]),
        pltpu.make_async_copy(low_ref, both_ref.at[pl.ds(0, half), 1 - core], sems.at[1]),
        pltpu.make_async_copy(high_ref, both_ref.at[pl.ds(half, half), 1 - core], sems.at[2]),
    ]
    for copy in copies:
        copy.start()
    for copy in copies:
        copy.wait()


def join(*parts):
    return pl.pallas_call(
        join_kernel,
        in_specs=[pl.BlockSpec(memory_space=pl.ANY)] * 3,
        out_specs=pl.BlockSpec(memory_space=pl.ANY),
        out_shape=jax.ShapeDtypeStruct((CHIPS, 2, SUB, LANES), BF),
        scratch_shapes=[pltpu.SemaphoreType.DMA((3,))],
        compiler_params=params(),
        cost_estimate=pl.CostEstimate(flops=0, bytes_accessed=0, transcendentals=0),
        name="join",
    )(*parts)


def gate_kernel(tiles_ref, _, out_ref):
    out_ref[...] = tiles_ref[...]


def gate(tiles, ready):
    return pl.pallas_call(
        gate_kernel,
        in_specs=[pl.BlockSpec(memory_space=pltpu.VMEM), pl.BlockSpec(memory_space=pl.ANY)],
        out_shape=jax.ShapeDtypeStruct(tiles.shape, BF),
        compiler_params=params(),
        name="gate",
    )(tiles, ready)


def block(ref):
    return ref[...].reshape(2 * GROUP, WIDTH)


def eye(size):
    return lax.broadcasted_iota(jnp.int32, (size, size), 0) == lax.broadcasted_iota(
        jnp.int32, (size, size), 1
    )


def live_of(rows):
    products = dot_t(rows, rows)
    down, across = [], []
    for start in range(0, rows.shape[0], LANES):
        part = products[start : start + LANES, start : start + LANES]
        diagonal = jnp.where(eye(LANES), part, NONE)
        down.append(jnp.max(diagonal, axis=1, keepdims=True) > 0.25)
        across.append(jnp.max(diagonal, axis=0, keepdims=True) > 0.25)
    return products, down, jnp.concatenate(across, axis=1)


def top(products, down, own=None):
    best = None
    for number, live in enumerate(down):
        part = products[number * LANES : (number + 1) * LANES]
        part = jnp.where(live & ~eye(LANES) if number == own else live, part, NONE)
        part = jnp.max(part, axis=0, keepdims=True)
        best = part if best is None else jnp.maximum(best, part)
    return best


def column_sum(products, down):
    total = None
    for number, live in enumerate(down):
        part = jnp.where(live, products[number * LANES : (number + 1) * LANES], 0.0)
        part = jnp.sum(part, axis=0, keepdims=True)
        total = part if total is None else total + part
    return total


def block_sum(rows, across):
    mask = jnp.broadcast_to(jnp.where(across, 1.0, 0.0), (8, rows.shape[0])).astype(BF)
    return dot(mask, rows)[0:1]


def first_kernel(mine_ref, near_ref, rows_ref):
    rows_ref[0] = block(mine_ref)
    rows_ref[1] = block(near_ref)


def first_two(mine, near):
    return pl.pallas_call(
        first_kernel,
        out_shape=jax.ShapeDtypeStruct((2, 2 * GROUP, WIDTH), BF),
        compiler_params=params(),
        name="first_two",
    )(mine, near)


def pairs_kernel(rows_ref, far_ref, best_ref, sums_ref, one_ref, two_ref):
    mine, near, far = rows_ref[0], rows_ref[1], block(far_ref)
    squares, mine_down, mine_across = live_of(mine)
    _, near_down, near_across = live_of(near)
    _, far_down, far_across = live_of(far)
    best = top(squares, mine_down, 0)
    best = jnp.maximum(best, top(dot_t(near, mine), near_down))
    best_ref[0:1] = jnp.maximum(best, top(dot_t(far, mine), far_down))
    best_ref[1:2] = jnp.where(mine_across, 1.0, 0.0)
    best_near = jnp.maximum(top(dot_t(mine, near), mine_down), top(dot_t(far, near), far_down))
    best_far = jnp.maximum(top(dot_t(mine, far), mine_down), top(dot_t(near, far), near_down))
    sum_mine = block_sum(mine, mine_across)
    sum_near = block_sum(near, near_across)
    sum_far = block_sum(far, far_across)
    sums_ref[0:1] = sum_mine
    sums_ref[1:2] = sum_near
    sums_ref[2:3] = sum_far
    one_ref[0:1] = sum_mine
    one_ref[1:2] = sum_far
    one_ref[2:3] = jnp.concatenate([best_near] * SUB, axis=1)
    two_ref[0:1] = sum_mine
    two_ref[1:2] = sum_near
    two_ref[2:3] = jnp.concatenate([best_far] * SUB, axis=1)


def pairs(rows, far):
    message = jax.ShapeDtypeStruct((3, WIDTH), F32)
    return pl.pallas_call(
        pairs_kernel,
        out_shape=[jax.ShapeDtypeStruct((2, 2 * GROUP), F32), message, message, message],
        compiler_params=params(),
        cost_estimate=LONG,
        name="pairs",
    )(rows, far)


def scale_of(total):
    return lax.rsqrt(jnp.sum(total * total) + EPS)


def products_with(total, rows):
    high, mid, low = three(total)
    parts = jnp.concatenate([high, mid, low, jnp.zeros((5, WIDTH), BF)], axis=0)
    found = dot_t(parts, rows)
    return found[0:1] + found[1:2] + found[2:3]


def early_kernel(rows_ref, best_ref, sums_ref, one_ref, two_ref, some_ref, held_ref):
    sign, col = sign_and_col()
    best = best_ref[0:1]
    for ref in (one_ref, two_ref):
        best = jnp.maximum(best, ref[2:3, : 2 * GROUP])
    held_ref[...] = jnp.zeros_like(held_ref)
    total = jnp.zeros((1, WIDTH), F32)
    for offset, row in (
        (0, sums_ref[0:1]),
        (1, sums_ref[1:2]),
        (3, sums_ref[2:3]),
        (7, one_ref[0:1]),
        (2, one_ref[1:2]),
        (5, two_ref[0:1]),
        (6, two_ref[1:2]),
    ):
        held_ref[pl.ds((col + sign * offset) & (N_COL - 1), 1)] = row
        total = total + row
    some_ref[0:1] = best
    some_ref[1:2] = products_with(total, rows_ref[0])
    some_ref[2:3] = best_ref[1:2]


def early(*operands):
    return pl.pallas_call(
        early_kernel,
        out_shape=[
            jax.ShapeDtypeStruct((3, 2 * GROUP), F32),
            jax.ShapeDtypeStruct((N_COL, WIDTH), F32),
        ],
        compiler_params=params(),
        name="early",
    )(*operands)


def giant_kernel(rows_ref, some_ref, held_ref, last_ref, max_ref, cos_ref, center_ref):
    sign, col = sign_and_col()
    last = block(last_ref)
    _, down, across = live_of(last)
    products = dot_t(last, rows_ref[0])
    place = (col + sign * 4) & (N_COL - 1)
    held = held_ref[...]
    is_last = lax.broadcasted_iota(jnp.int32, held.shape, 0) == place
    held = jnp.where(is_last, block_sum(last, across), held)
    total = held[0:1]
    for number in range(1, N_COL):
        total = total + held[number : number + 1]
    scale = scale_of(total)
    live = some_ref[2:3] > 0.0
    max_ref[...] = jnp.where(live, jnp.maximum(some_ref[0:1], top(products, down)), 0.0)
    cos_ref[...] = jnp.where(live, (some_ref[1:2] + column_sum(products, down)) * scale, 0.0)
    center_ref[...] = total * scale


def normal_kernel(tiles_ref, max_ref, cos_ref, center_ref, rows_ref):
    for y in range(CHIPS // RUN):
        for core in range(2):
            start = (2 * y + core) * RUN
            rows_ref[start : start + RUN] = tiles_ref[y * RUN : (y + 1) * RUN, core].reshape(
                RUN, WIDTH
            )
    rows = rows_ref[...]
    products, down, across = live_of(rows)
    total = block_sum(rows, across)
    scale = scale_of(total)
    center_ref[...] = total * scale
    best = [
        top(products[:, number * LANES : (number + 1) * LANES], down, number)
        for number in range(len(down))
    ]
    max_ref[...] = jnp.where(across, jnp.concatenate(best, axis=1), 0.0)
    cos_ref[...] = jnp.where(across, column_sum(products, down) * scale, 0.0)


def row(size):
    return jax.ShapeDtypeStruct((1, size), F32)


def giant_stats(*operands):
    return pl.pallas_call(
        giant_kernel,
        out_shape=[row(2 * GROUP), row(2 * GROUP), row(WIDTH)],
        compiler_params=params(),
        name="giants",
    )(*operands)


def normal_stats(tiles):
    return pl.pallas_call(
        normal_kernel,
        out_shape=[row(OWNERS), row(OWNERS), row(WIDTH)],
        scratch_shapes=[pltpu.VMEM((OWNERS, WIDTH), BF)],
        compiler_params=params(),
        name="ordinary",
    )(tiles)


def along(rows, offset):
    moves = []
    for src in range(N_SRC):
        for col in range(N_COL):
            goal = (col + (offset if src % 2 == 0 else -offset)) % N_COL
            moves.append((src * N_COL + col, src * N_COL + goal))
    return lax.ppermute(rows, ("y", "core", "col"), moves)


def to_other_core(rows):
    return lax.ppermute(rows, "core", [(0, 1), (1, 0)])


def all_to_all(rows, axes):
    return lax.all_to_all(rows, axes, split_axis=0, concat_axis=0, tiled=True)


def per_device(embed, assign, slot):
    giant, lines = giant_pack(embed, assign, slot)
    giant = all_to_all(giant, ("y", "core", "clu"))
    same, low, high = pack(embed, lines)
    both = join(same, to_other_core(low), to_other_core(high))
    mine = gate(giant, both)
    near, far = along(mine, 7), along(mine, 5)
    both = all_to_all(both, ("y", "clu", "col"))
    last = along(far, 7)
    rows = first_two(mine, near)
    best, sums, one, two = pairs(rows, far)
    one, two = along(one, 1), along(two, 3)
    some, held = early(rows, best, sums, one, two)
    giants = giant_stats(rows, some, held, last)
    return (*normal_stats(both), *giants)


def solution(mesh):
    fine = Mesh(mesh.devices.reshape(N_SRC // 2, 2, -1, N_COL), ("y", "core", "clu", "col"))
    plane = ("y", "core", "clu")
    everywhere = (*plane, "col")
    in_specs = (P(everywhere, None), P(everywhere), P(everywhere))
    out_specs = (
        P(everywhere, None),
        P(everywhere, None),
        P(everywhere, None),
        P(plane, "col"),
        P(plane, "col"),
        P(plane, None),
    )
    return jax.shard_map(
        per_device, mesh=fine, in_specs=in_specs, out_specs=out_specs, check_vma=False
    )
```

```python
import jax
import jax.numpy as jnp
from jax import lax
from jax.experimental import pallas as pl
from jax.experimental.pallas import tpu as pltpu
from jax.sharding import Mesh
from jax.sharding import PartitionSpec as P

N_COL = 8
N_SRC = 16
GROUP = 64
OWNERS = GROUP * N_COL
CHIPS = OWNERS // 2
RUN = 32
WIDTH = 1024
LANES = 128
SUB = WIDTH // LANES
EPS = 1e-06
NONE = -4.0

BF = jnp.bfloat16
F32 = jnp.float32


LONG = pl.CostEstimate(flops=30_000_000_000, bytes_accessed=2_000_000, transcendentals=0)


def params(mib=12):
    return pltpu.CompilerParams(vmem_limit_bytes=mib * 1024 * 1024)


def dot_t(left, right):
    return lax.dot_general(left, right, (((1,), (1,)), ((), ())), preferred_element_type=F32)


def dot(left, right):
    return jnp.dot(left, right, preferred_element_type=F32)


def three(values):
    high = values.astype(BF)
    rest = values - high.astype(F32)
    mid = rest.astype(BF)
    low = (rest - mid.astype(F32)).astype(BF)
    return high, mid, low


def sign_and_col():
    return 1 - 2 * lax.axis_index("core"), lax.axis_index("col")


def unit_rows(rows):
    values = rows.astype(F32)
    return (values * lax.rsqrt(jnp.sum(values * values, axis=1, keepdims=True) + EPS)).astype(BF)


def placed(rows, target, start, count):
    places = lax.broadcasted_iota(jnp.int32, (count, target.shape[1]), 0) + start
    pick = jnp.where(places == target, 1.0, 0.0).astype(BF)
    return dot(pick, rows).astype(BF)


def giant_pack_kernel(
    embed_hbm, assign_hbm, slot_hbm, giant_ref, lines_ref, embed_ref, assign_ref, slot_ref, sems
):
    parts = (pl.ds(0, LANES), pl.ds(LANES, embed_ref.shape[0] - LANES))
    copies = [
        pltpu.make_async_copy(assign_hbm, assign_ref, sems.at[0]),
        pltpu.make_async_copy(slot_hbm, slot_ref, sems.at[1]),
    ]
    copies += [
        pltpu.make_async_copy(embed_hbm.at[part], embed_ref.at[part], sems.at[2 + number])
        for number, part in enumerate(parts)
    ]
    for copy in copies:
        copy.start()
    copies[0].wait()
    copies[1].wait()
    assign = assign_ref[...].reshape(1, -1)
    lines_ref[...] = assign
    target = (slot_ref[...].reshape(1, -1) & 1) * GROUP + assign - OWNERS
    target = jnp.where(assign >= OWNERS, target, -1)
    places = lax.broadcasted_iota(jnp.int32, (2 * GROUP, target.shape[1]), 0)
    pick = jnp.where(places == target, 1.0, 0.0).astype(BF)
    copies[2].wait()
    rows = dot(pick[:, :LANES], embed_ref[:LANES])
    copies[3].wait()
    rows = unit_rows(rows + dot(pick[:, LANES:], embed_ref[LANES:]))
    for number in range(2):
        part = rows[number * GROUP : (number + 1) * GROUP]
        giant_ref[:, number] = part.reshape(GROUP, SUB, LANES)


def giant_pack(embed, assign, slot):
    return pl.pallas_call(
        giant_pack_kernel,
        in_specs=[pl.BlockSpec(memory_space=pl.ANY)] * 3,
        out_shape=[
            jax.ShapeDtypeStruct((GROUP, 2, SUB, LANES), BF),
            jax.ShapeDtypeStruct((1, assign.shape[0]), jnp.int32),
        ],
        scratch_shapes=[
            pltpu.VMEM(embed.shape, BF),
            pltpu.VMEM(assign.shape, jnp.int32),
            pltpu.VMEM(slot.shape, jnp.int32),
            pltpu.SemaphoreType.DMA((4,)),
        ],
        compiler_params=params(56),
        name="giant_pack",
    )(embed, assign, slot)


def pack_kernel(embed_ref, assign_ref, same_ref, *other_refs):
    core = lax.axis_index("core")
    assign = assign_ref[...]
    chip = (assign // (2 * RUN)) * RUN + (assign & (RUN - 1))
    other = ((assign // RUN) & 1) != core
    target = jnp.where(assign >= OWNERS, -1, jnp.where(other, CHIPS, 0) + chip)
    unit = unit_rows(embed_ref[...])
    half = CHIPS // 2
    for number, ref in enumerate(other_refs):
        rows = placed(unit, target, CHIPS + number * half, half)
        ref[...] = rows.reshape(half, SUB, LANES)
    for start in (0, half):
        rows = placed(unit, target, start, half)
        same_ref[start : start + half] = rows.reshape(half, SUB, LANES)


def pack(embed, assign):
    shape = lambda rows: jax.ShapeDtypeStruct((rows, SUB, LANES), BF)
    return pl.pallas_call(
        pack_kernel,
        out_shape=[shape(CHIPS), shape(CHIPS // 2), shape(CHIPS // 2)],
        compiler_params=params(),
        name="pack",
    )(embed, assign)


def join_kernel(same_ref, low_ref, high_ref, both_ref, sems):
    core = lax.axis_index("core")
    half = CHIPS // 2
    copies = [
        pltpu.make_async_copy(same_ref, both_ref.at[:, core], sems.at[0]),
        pltpu.make_async_copy(low_ref, both_ref.at[pl.ds(0, half), 1 - core], sems.at[1]),
        pltpu.make_async_copy(high_ref, both_ref.at[pl.ds(half, half), 1 - core], sems.at[2]),
    ]
    for copy in copies:
        copy.start()
    for copy in copies:
        copy.wait()


def join(*parts):
    return pl.pallas_call(
        join_kernel,
        in_specs=[pl.BlockSpec(memory_space=pl.ANY)] * 3,
        out_specs=pl.BlockSpec(memory_space=pl.ANY),
        out_shape=jax.ShapeDtypeStruct((CHIPS, 2, SUB, LANES), BF),
        scratch_shapes=[pltpu.SemaphoreType.DMA((3,))],
        compiler_params=params(),
        cost_estimate=pl.CostEstimate(flops=0, bytes_accessed=0, transcendentals=0),
        name="join",
    )(*parts)


def gate_kernel(tiles_ref, _, out_ref):
    out_ref[...] = tiles_ref[...]


def gate(tiles, ready):
    return pl.pallas_call(
        gate_kernel,
        in_specs=[pl.BlockSpec(memory_space=pltpu.VMEM), pl.BlockSpec(memory_space=pl.ANY)],
        out_shape=jax.ShapeDtypeStruct(tiles.shape, BF),
        compiler_params=params(),
        name="gate",
    )(tiles, ready)


def block(ref):
    return ref[...].reshape(2 * GROUP, WIDTH)


def eye(size):
    return lax.broadcasted_iota(jnp.int32, (size, size), 0) == lax.broadcasted_iota(
        jnp.int32, (size, size), 1
    )


def live_of(rows):
    products = dot_t(rows, rows)
    down, across = [], []
    for start in range(0, rows.shape[0], LANES):
        part = products[start : start + LANES, start : start + LANES]
        diagonal = jnp.where(eye(LANES), part, NONE)
        down.append(jnp.max(diagonal, axis=1, keepdims=True) > 0.25)
        across.append(jnp.max(diagonal, axis=0, keepdims=True) > 0.25)
    return products, down, jnp.concatenate(across, axis=1)


def top(products, down, own=None):
    best = None
    for number, live in enumerate(down):
        part = products[number * LANES : (number + 1) * LANES]
        part = jnp.where(live & ~eye(LANES) if number == own else live, part, NONE)
        part = jnp.max(part, axis=0, keepdims=True)
        best = part if best is None else jnp.maximum(best, part)
    return best


def column_sum(products, down):
    total = None
    for number, live in enumerate(down):
        part = jnp.where(live, products[number * LANES : (number + 1) * LANES], 0.0)
        part = jnp.sum(part, axis=0, keepdims=True)
        total = part if total is None else total + part
    return total


def block_sum(rows, across):
    mask = jnp.broadcast_to(jnp.where(across, 1.0, 0.0), (8, rows.shape[0])).astype(BF)
    return dot(mask, rows)[0:1]


def first_kernel(mine_ref, near_ref, rows_ref):
    rows_ref[0] = block(mine_ref)
    rows_ref[1] = block(near_ref)


def first_two(mine, near):
    return pl.pallas_call(
        first_kernel,
        out_shape=jax.ShapeDtypeStruct((2, 2 * GROUP, WIDTH), BF),
        compiler_params=params(),
        name="first_two",
    )(mine, near)


def pairs_kernel(rows_ref, far_ref, best_ref, sums_ref, one_ref, two_ref):
    mine, near, far = rows_ref[0], rows_ref[1], block(far_ref)
    squares, mine_down, mine_across = live_of(mine)
    _, near_down, near_across = live_of(near)
    _, far_down, far_across = live_of(far)
    best = top(squares, mine_down, 0)
    best = jnp.maximum(best, top(dot_t(near, mine), near_down))
    best_ref[0:1] = jnp.maximum(best, top(dot_t(far, mine), far_down))
    best_ref[1:2] = jnp.where(mine_across, 1.0, 0.0)
    best_near = jnp.maximum(top(dot_t(mine, near), mine_down), top(dot_t(far, near), far_down))
    best_far = jnp.maximum(top(dot_t(mine, far), mine_down), top(dot_t(near, far), near_down))
    sum_mine = block_sum(mine, mine_across)
    sum_near = block_sum(near, near_across)
    sum_far = block_sum(far, far_across)
    sums_ref[0:1] = sum_mine
    sums_ref[1:2] = sum_near
    sums_ref[2:3] = sum_far
    one_ref[0:1] = sum_mine
    one_ref[1:2] = sum_far
    one_ref[2:3] = jnp.concatenate([best_near] * SUB, axis=1)
    two_ref[0:1] = sum_mine
    two_ref[1:2] = sum_near
    two_ref[2:3] = jnp.concatenate([best_far] * SUB, axis=1)


def pairs(rows, far):
    message = jax.ShapeDtypeStruct((3, WIDTH), F32)
    return pl.pallas_call(
        pairs_kernel,
        out_shape=[jax.ShapeDtypeStruct((2, 2 * GROUP), F32), message, message, message],
        compiler_params=params(),
        cost_estimate=LONG,
        name="pairs",
    )(rows, far)


def scale_of(total):
    return lax.rsqrt(jnp.sum(total * total) + EPS)


def products_with(total, rows):
    high, mid, low = three(total)
    parts = jnp.concatenate([high, mid, low, jnp.zeros((5, WIDTH), BF)], axis=0)
    found = dot_t(parts, rows)
    return found[0:1] + found[1:2] + found[2:3]


def early_kernel(rows_ref, best_ref, sums_ref, one_ref, two_ref, some_ref, held_ref):
    sign, col = sign_and_col()
    best = best_ref[0:1]
    for ref in (one_ref, two_ref):
        best = jnp.maximum(best, ref[2:3, : 2 * GROUP])
    held_ref[...] = jnp.zeros_like(held_ref)
    total = jnp.zeros((1, WIDTH), F32)
    for offset, row in (
        (0, sums_ref[0:1]),
        (1, sums_ref[1:2]),
        (6, sums_ref[2:3]),
        (7, one_ref[0:1]),
        (5, one_ref[1:2]),
        (2, two_ref[0:1]),
        (3, two_ref[1:2]),
    ):
        held_ref[pl.ds((col + sign * offset) & (N_COL - 1), 1)] = row
        total = total + row
    some_ref[0:1] = best
    some_ref[1:2] = products_with(total, rows_ref[0])
    some_ref[2:3] = best_ref[1:2]


def early(*operands):
    return pl.pallas_call(
        early_kernel,
        out_shape=[
            jax.ShapeDtypeStruct((3, 2 * GROUP), F32),
            jax.ShapeDtypeStruct((N_COL, WIDTH), F32),
        ],
        compiler_params=params(),
        name="early",
    )(*operands)


def giant_kernel(rows_ref, some_ref, held_ref, last_ref, max_ref, cos_ref, center_ref):
    sign, col = sign_and_col()
    last = block(last_ref)
    _, down, across = live_of(last)
    products = dot_t(last, rows_ref[0])
    place = (col + sign * 4) & (N_COL - 1)
    held = held_ref[...]
    is_last = lax.broadcasted_iota(jnp.int32, held.shape, 0) == place
    held = jnp.where(is_last, block_sum(last, across), held)
    total = held[0:1]
    for number in range(1, N_COL):
        total = total + held[number : number + 1]
    scale = scale_of(total)
    live = some_ref[2:3] > 0.0
    max_ref[...] = jnp.where(live, jnp.maximum(some_ref[0:1], top(products, down)), 0.0)
    cos_ref[...] = jnp.where(live, (some_ref[1:2] + column_sum(products, down)) * scale, 0.0)
    center_ref[...] = total * scale


def normal_kernel(tiles_ref, max_ref, cos_ref, center_ref, rows_ref):
    for y in range(CHIPS // RUN):
        for core in range(2):
            start = (2 * y + core) * RUN
            rows_ref[start : start + RUN] = tiles_ref[y * RUN : (y + 1) * RUN, core].reshape(
                RUN, WIDTH
            )
    rows = rows_ref[...]
    products, down, across = live_of(rows)
    total = block_sum(rows, across)
    scale = scale_of(total)
    center_ref[...] = total * scale
    best = [
        top(products[:, number * LANES : (number + 1) * LANES], down, number)
        for number in range(len(down))
    ]
    max_ref[...] = jnp.where(across, jnp.concatenate(best, axis=1), 0.0)
    cos_ref[...] = jnp.where(across, column_sum(products, down) * scale, 0.0)


def tail_kernel(tiles_ref, rows_ref, some_ref, held_ref, last_ref, *refs):
    *outs, scratch_ref = refs
    giant_kernel(rows_ref, some_ref, held_ref, last_ref, *outs[3:])
    normal_kernel(tiles_ref, *outs[:3], scratch_ref)


def tail(*operands):
    row = lambda size: jax.ShapeDtypeStruct((1, size), F32)
    return pl.pallas_call(
        tail_kernel,
        out_shape=[row(OWNERS), row(OWNERS), row(WIDTH), row(2 * GROUP), row(2 * GROUP), row(WIDTH)],
        scratch_shapes=[pltpu.VMEM((OWNERS, WIDTH), BF)],
        compiler_params=params(),
        name="tail",
    )(*operands)


def along(rows, offset):
    moves = []
    for src in range(N_SRC):
        for col in range(N_COL):
            goal = (col + (offset if src % 2 == 0 else -offset)) % N_COL
            moves.append((src * N_COL + col, src * N_COL + goal))
    return lax.ppermute(rows, ("y", "core", "col"), moves)


def to_other_core(rows):
    return lax.ppermute(rows, "core", [(0, 1), (1, 0)])


def all_to_all(rows, axes):
    return lax.all_to_all(rows, axes, split_axis=0, concat_axis=0, tiled=True)


def per_device(embed, assign, slot):
    giant, lines = giant_pack(embed, assign, slot)
    giant = all_to_all(giant, ("y", "core", "clu"))
    same, low, high = pack(embed, lines)
    both = join(same, to_other_core(low), to_other_core(high))
    mine = gate(giant, both)
    near, far = along(mine, 7), along(mine, 2)
    both = all_to_all(both, ("y", "clu", "col"))
    last = along(far, 2)
    rows = first_two(mine, near)
    best, sums, one, two = pairs(rows, far)
    one, two = along(one, 1), along(two, 6)
    some, held = early(rows, best, sums, one, two)
    return tuple(tail(both, rows, some, held, last))


def solution(mesh):
    fine = Mesh(mesh.devices.reshape(N_SRC // 2, 2, -1, N_COL), ("y", "core", "clu", "col"))
    plane = ("y", "core", "clu")
    everywhere = (*plane, "col")
    in_specs = (P(everywhere, None), P(everywhere), P(everywhere))
    out_specs = (
        P(everywhere, None),
        P(everywhere, None),
        P(everywhere, None),
        P(plane, "col"),
        P(plane, "col"),
        P(plane, None),
    )
    return jax.shard_map(
        per_device, mesh=fine, in_specs=in_specs, out_specs=out_specs, check_vma=False
    )
```

```python
import jax
import jax.numpy as jnp
from jax import lax
from jax.experimental import pallas as pl
from jax.experimental.pallas import tpu as pltpu
from jax.sharding import Mesh
from jax.sharding import PartitionSpec as P

N_COL = 8
N_SRC = 16
GROUP = 64
OWNERS = GROUP * N_COL
CHIPS = OWNERS // 2
RUN = 32
WIDTH = 1024
LANES = 128
SUB = WIDTH // LANES
EPS = 1e-06
NONE = -4.0

BF = jnp.bfloat16
F32 = jnp.float32


LONG = pl.CostEstimate(flops=30_000_000_000, bytes_accessed=2_000_000, transcendentals=0)


def params(mib=12):
    return pltpu.CompilerParams(vmem_limit_bytes=mib * 1024 * 1024)


def dot_t(left, right):
    return lax.dot_general(left, right, (((1,), (1,)), ((), ())), preferred_element_type=F32)


def dot(left, right):
    return jnp.dot(left, right, preferred_element_type=F32)


def three(values):
    high = values.astype(BF)
    rest = values - high.astype(F32)
    mid = rest.astype(BF)
    low = (rest - mid.astype(F32)).astype(BF)
    return high, mid, low


def sign_and_col():
    return 1 - 2 * lax.axis_index("core"), lax.axis_index("col")


def unit_rows(rows):
    values = rows.astype(F32)
    return (values * lax.rsqrt(jnp.sum(values * values, axis=1, keepdims=True) + EPS)).astype(BF)


def placed(rows, target, start, count):
    places = lax.broadcasted_iota(jnp.int32, (count, target.shape[1]), 0) + start
    pick = jnp.where(places == target, 1.0, 0.0).astype(BF)
    return dot(pick, rows).astype(BF)


def giant_pack_kernel(
    embed_hbm, assign_hbm, slot_hbm, giant_ref, lines_ref, embed_ref, assign_ref, slot_ref, sems
):
    parts = (pl.ds(0, LANES), pl.ds(LANES, embed_ref.shape[0] - LANES))
    copies = [
        pltpu.make_async_copy(assign_hbm, assign_ref, sems.at[0]),
        pltpu.make_async_copy(slot_hbm, slot_ref, sems.at[1]),
    ]
    copies += [
        pltpu.make_async_copy(embed_hbm.at[part], embed_ref.at[part], sems.at[2 + number])
        for number, part in enumerate(parts)
    ]
    for copy in copies:
        copy.start()
    copies[0].wait()
    copies[1].wait()
    assign = assign_ref[...].reshape(1, -1)
    lines_ref[...] = assign
    target = (slot_ref[...].reshape(1, -1) & 1) * GROUP + assign - OWNERS
    target = jnp.where(assign >= OWNERS, target, -1)
    places = lax.broadcasted_iota(jnp.int32, (2 * GROUP, target.shape[1]), 0)
    pick = jnp.where(places == target, 1.0, 0.0).astype(BF)
    copies[2].wait()
    rows = dot(pick[:, :LANES], embed_ref[:LANES])
    copies[3].wait()
    rows = (rows + dot(pick[:, LANES:], embed_ref[LANES:])).astype(BF)
    for number in range(2):
        part = rows[number * GROUP : (number + 1) * GROUP]
        giant_ref[:, number] = part.reshape(GROUP, SUB, LANES)


def giant_pack(embed, assign, slot):
    return pl.pallas_call(
        giant_pack_kernel,
        in_specs=[pl.BlockSpec(memory_space=pl.ANY)] * 3,
        out_shape=[
            jax.ShapeDtypeStruct((GROUP, 2, SUB, LANES), BF),
            jax.ShapeDtypeStruct((1, assign.shape[0]), jnp.int32),
        ],
        scratch_shapes=[
            pltpu.VMEM(embed.shape, BF),
            pltpu.VMEM(assign.shape, jnp.int32),
            pltpu.VMEM(slot.shape, jnp.int32),
            pltpu.SemaphoreType.DMA((4,)),
        ],
        compiler_params=params(56),
        name="giant_pack",
    )(embed, assign, slot)


def pack_kernel(embed_ref, assign_ref, same_ref, *other_refs):
    core = lax.axis_index("core")
    assign = assign_ref[...]
    chip = (assign // (2 * RUN)) * RUN + (assign & (RUN - 1))
    other = ((assign // RUN) & 1) != core
    target = jnp.where(assign >= OWNERS, -1, jnp.where(other, CHIPS, 0) + chip)
    unit = unit_rows(embed_ref[...])
    half = CHIPS // 2
    for number, ref in enumerate(other_refs):
        rows = placed(unit, target, CHIPS + number * half, half)
        ref[...] = rows.reshape(half, SUB, LANES)
    for start in (0, half):
        rows = placed(unit, target, start, half)
        same_ref[start : start + half] = rows.reshape(half, SUB, LANES)


def pack(embed, assign):
    shape = lambda rows: jax.ShapeDtypeStruct((rows, SUB, LANES), BF)
    return pl.pallas_call(
        pack_kernel,
        out_shape=[shape(CHIPS), shape(CHIPS // 2), shape(CHIPS // 2)],
        compiler_params=params(),
        name="pack",
    )(embed, assign)


def join_kernel(same_ref, low_ref, high_ref, both_ref, sems):
    core = lax.axis_index("core")
    half = CHIPS // 2
    copies = [
        pltpu.make_async_copy(same_ref, both_ref.at[:, core], sems.at[0]),
        pltpu.make_async_copy(low_ref, both_ref.at[pl.ds(0, half), 1 - core], sems.at[1]),
        pltpu.make_async_copy(high_ref, both_ref.at[pl.ds(half, half), 1 - core], sems.at[2]),
    ]
    for copy in copies:
        copy.start()
    for copy in copies:
        copy.wait()


def join(*parts):
    return pl.pallas_call(
        join_kernel,
        in_specs=[pl.BlockSpec(memory_space=pl.ANY)] * 3,
        out_specs=pl.BlockSpec(memory_space=pl.ANY),
        out_shape=jax.ShapeDtypeStruct((CHIPS, 2, SUB, LANES), BF),
        scratch_shapes=[pltpu.SemaphoreType.DMA((3,))],
        compiler_params=params(),
        cost_estimate=pl.CostEstimate(flops=0, bytes_accessed=0, transcendentals=0),
        name="join",
    )(*parts)


def gate_kernel(tiles_ref, _, out_ref):
    out_ref[...] = tiles_ref[...]


def gate(tiles, ready):
    return pl.pallas_call(
        gate_kernel,
        in_specs=[pl.BlockSpec(memory_space=pltpu.VMEM), pl.BlockSpec(memory_space=pl.ANY)],
        out_shape=jax.ShapeDtypeStruct(tiles.shape, BF),
        compiler_params=params(),
        name="gate",
    )(tiles, ready)


def block(ref):
    return ref[...].reshape(2 * GROUP, WIDTH)


def eye(size):
    return lax.broadcasted_iota(jnp.int32, (size, size), 0) == lax.broadcasted_iota(
        jnp.int32, (size, size), 1
    )


def live_of(rows):
    products = dot_t(rows, rows)
    down, across = [], []
    for start in range(0, rows.shape[0], LANES):
        part = products[start : start + LANES, start : start + LANES]
        diagonal = jnp.where(eye(LANES), part, NONE)
        down.append(jnp.max(diagonal, axis=1, keepdims=True) > 0.25)
        across.append(jnp.max(diagonal, axis=0, keepdims=True) > 0.25)
    return products, down, jnp.concatenate(across, axis=1)


def top(products, down, own=None):
    best = None
    for number, live in enumerate(down):
        part = products[number * LANES : (number + 1) * LANES]
        part = jnp.where(live & ~eye(LANES) if number == own else live, part, NONE)
        part = jnp.max(part, axis=0, keepdims=True)
        best = part if best is None else jnp.maximum(best, part)
    return best


def column_sum(products, down):
    total = None
    for number, live in enumerate(down):
        part = jnp.where(live, products[number * LANES : (number + 1) * LANES], 0.0)
        part = jnp.sum(part, axis=0, keepdims=True)
        total = part if total is None else total + part
    return total


def block_sum(rows, across):
    mask = jnp.broadcast_to(jnp.where(across, 1.0, 0.0), (8, rows.shape[0])).astype(BF)
    return dot(mask, rows)[0:1]


def first_kernel(mine_ref, near_ref, far_ref, rows_ref, unit_ref):
    rows_ref[0] = unit_rows(block(mine_ref))
    rows_ref[1] = unit_rows(block(near_ref))
    far = unit_rows(block(far_ref))
    rows_ref[2] = far
    unit_ref[...] = far.reshape(unit_ref.shape)


def unit_blocks(mine, near, far):
    return pl.pallas_call(
        first_kernel,
        out_shape=[
            jax.ShapeDtypeStruct((3, 2 * GROUP, WIDTH), BF),
            jax.ShapeDtypeStruct(far.shape, BF),
        ],
        compiler_params=params(),
        name="unit_blocks",
    )(mine, near, far)


def pairs_kernel(rows_ref, best_ref, sums_ref, one_ref, two_ref):
    mine, near, far = rows_ref[0], rows_ref[1], rows_ref[2]
    squares, mine_down, mine_across = live_of(mine)
    _, near_down, near_across = live_of(near)
    _, far_down, far_across = live_of(far)
    best = top(squares, mine_down, 0)
    best = jnp.maximum(best, top(dot_t(near, mine), near_down))
    best_ref[0:1] = jnp.maximum(best, top(dot_t(far, mine), far_down))
    best_ref[1:2] = jnp.where(mine_across, 1.0, 0.0)
    best_near = jnp.maximum(top(dot_t(mine, near), mine_down), top(dot_t(far, near), far_down))
    best_far = jnp.maximum(top(dot_t(mine, far), mine_down), top(dot_t(near, far), near_down))
    sum_mine = block_sum(mine, mine_across)
    sum_near = block_sum(near, near_across)
    sum_far = block_sum(far, far_across)
    sums_ref[0:1] = sum_mine
    sums_ref[1:2] = sum_near
    sums_ref[2:3] = sum_far
    one_ref[0:1] = sum_mine
    one_ref[1:2] = sum_far
    one_ref[2:3] = jnp.concatenate([best_near] * SUB, axis=1)
    two_ref[0:1] = sum_mine
    two_ref[1:2] = sum_near
    two_ref[2:3] = jnp.concatenate([best_far] * SUB, axis=1)


def pairs(rows):
    message = jax.ShapeDtypeStruct((3, WIDTH), F32)
    return pl.pallas_call(
        pairs_kernel,
        out_shape=[jax.ShapeDtypeStruct((2, 2 * GROUP), F32), message, message, message],
        compiler_params=params(),
        cost_estimate=LONG,
        name="pairs",
    )(rows)


def scale_of(total):
    return lax.rsqrt(jnp.sum(total * total) + EPS)


def products_with(total, rows):
    high, mid, low = three(total)
    parts = jnp.concatenate([high, mid, low, jnp.zeros((5, WIDTH), BF)], axis=0)
    found = dot_t(parts, rows)
    return found[0:1] + found[1:2] + found[2:3]


def early_kernel(rows_ref, best_ref, sums_ref, one_ref, two_ref, some_ref, held_ref):
    sign, col = sign_and_col()
    best = best_ref[0:1]
    for ref in (one_ref, two_ref):
        best = jnp.maximum(best, ref[2:3, : 2 * GROUP])
    held_ref[...] = jnp.zeros_like(held_ref)
    total = jnp.zeros((1, WIDTH), F32)
    for offset, row in (
        (0, sums_ref[0:1]),
        (1, sums_ref[1:2]),
        (6, sums_ref[2:3]),
        (7, one_ref[0:1]),
        (5, one_ref[1:2]),
        (2, two_ref[0:1]),
        (3, two_ref[1:2]),
    ):
        held_ref[pl.ds((col + sign * offset) & (N_COL - 1), 1)] = row
        total = total + row
    some_ref[0:1] = best
    some_ref[1:2] = products_with(total, rows_ref[0])
    some_ref[2:3] = best_ref[1:2]


def early(*operands):
    return pl.pallas_call(
        early_kernel,
        out_shape=[
            jax.ShapeDtypeStruct((3, 2 * GROUP), F32),
            jax.ShapeDtypeStruct((N_COL, WIDTH), F32),
        ],
        compiler_params=params(),
        name="early",
    )(*operands)


def giant_kernel(rows_ref, some_ref, held_ref, last_ref, max_ref, cos_ref, center_ref):
    sign, col = sign_and_col()
    last = block(last_ref)
    _, down, across = live_of(last)
    products = dot_t(last, rows_ref[0])
    place = (col + sign * 4) & (N_COL - 1)
    held = held_ref[...]
    is_last = lax.broadcasted_iota(jnp.int32, held.shape, 0) == place
    held = jnp.where(is_last, block_sum(last, across), held)
    total = held[0:1]
    for number in range(1, N_COL):
        total = total + held[number : number + 1]
    scale = scale_of(total)
    live = some_ref[2:3] > 0.0
    max_ref[...] = jnp.where(live, jnp.maximum(some_ref[0:1], top(products, down)), 0.0)
    cos_ref[...] = jnp.where(live, (some_ref[1:2] + column_sum(products, down)) * scale, 0.0)
    center_ref[...] = total * scale


def normal_kernel(tiles_ref, max_ref, cos_ref, center_ref, rows_ref):
    for y in range(CHIPS // RUN):
        for core in range(2):
            start = (2 * y + core) * RUN
            rows_ref[start : start + RUN] = tiles_ref[y * RUN : (y + 1) * RUN, core].reshape(
                RUN, WIDTH
            )
    rows = rows_ref[...]
    products, down, across = live_of(rows)
    total = block_sum(rows, across)
    scale = scale_of(total)
    center_ref[...] = total * scale
    best = [
        top(products[:, number * LANES : (number + 1) * LANES], down, number)
        for number in range(len(down))
    ]
    max_ref[...] = jnp.where(across, jnp.concatenate(best, axis=1), 0.0)
    cos_ref[...] = jnp.where(across, column_sum(products, down) * scale, 0.0)


def tail_kernel(tiles_ref, rows_ref, some_ref, held_ref, last_ref, *refs):
    *outs, scratch_ref = refs
    giant_kernel(rows_ref, some_ref, held_ref, last_ref, *outs[3:])
    normal_kernel(tiles_ref, *outs[:3], scratch_ref)


def tail(*operands):
    row = lambda size: jax.ShapeDtypeStruct((1, size), F32)
    return pl.pallas_call(
        tail_kernel,
        out_shape=[row(OWNERS), row(OWNERS), row(WIDTH), row(2 * GROUP), row(2 * GROUP), row(WIDTH)],
        scratch_shapes=[pltpu.VMEM((OWNERS, WIDTH), BF)],
        compiler_params=params(),
        name="tail",
    )(*operands)


def along(rows, offset):
    moves = []
    for src in range(N_SRC):
        for col in range(N_COL):
            goal = (col + (offset if src % 2 == 0 else -offset)) % N_COL
            moves.append((src * N_COL + col, src * N_COL + goal))
    return lax.ppermute(rows, ("y", "core", "col"), moves)


def to_other_core(rows):
    return lax.ppermute(rows, "core", [(0, 1), (1, 0)])


def all_to_all(rows, axes):
    return lax.all_to_all(rows, axes, split_axis=0, concat_axis=0, tiled=True)


def per_device(embed, assign, slot):
    giant, lines = giant_pack(embed, assign, slot)
    giant = all_to_all(giant, ("y", "core", "clu"))
    same, low, high = pack(embed, lines)
    both = join(same, to_other_core(low), to_other_core(high))
    mine = gate(giant, both)
    near, far = along(mine, 7), along(mine, 2)
    both = all_to_all(both, ("y", "clu", "col"))
    rows, far = unit_blocks(mine, near, far)
    last = along(far, 2)
    best, sums, one, two = pairs(rows)
    one, two = along(one, 1), along(two, 6)
    some, held = early(rows, best, sums, one, two)
    return tuple(tail(both, rows, some, held, last))


def solution(mesh):
    fine = Mesh(mesh.devices.reshape(N_SRC // 2, 2, -1, N_COL), ("y", "core", "clu", "col"))
    plane = ("y", "core", "clu")
    everywhere = (*plane, "col")
    in_specs = (P(everywhere, None), P(everywhere), P(everywhere))
    out_specs = (
        P(everywhere, None),
        P(everywhere, None),
        P(everywhere, None),
        P(plane, "col"),
        P(plane, "col"),
        P(plane, None),
    )
    return jax.shard_map(
        per_device, mesh=fine, in_specs=in_specs, out_specs=out_specs, check_vma=False
    )
```

```python
import jax
import jax.numpy as jnp
from jax import lax
from jax.experimental import pallas as pl
from jax.experimental.pallas import tpu as pltpu
from jax.sharding import Mesh
from jax.sharding import PartitionSpec as P

N_COL = 8
N_SRC = 16
GROUP = 64
OWNERS = GROUP * N_COL
CHIPS = OWNERS // 2
RUN = 32
WIDTH = 1024
LANES = 128
SUB = WIDTH // LANES
EPS = 1e-06
NONE = -4.0

BF = jnp.bfloat16
F32 = jnp.float32


LONG = pl.CostEstimate(flops=30_000_000_000, bytes_accessed=2_000_000, transcendentals=0)


def params(mib=12):
    return pltpu.CompilerParams(vmem_limit_bytes=mib * 1024 * 1024)


def dot_t(left, right):
    return lax.dot_general(left, right, (((1,), (1,)), ((), ())), preferred_element_type=F32)


def dot(left, right):
    return jnp.dot(left, right, preferred_element_type=F32)


def three(values):
    high = values.astype(BF)
    rest = values - high.astype(F32)
    mid = rest.astype(BF)
    low = (rest - mid.astype(F32)).astype(BF)
    return high, mid, low


def sign_and_col():
    return 1 - 2 * lax.axis_index("core"), lax.axis_index("col")


def unit_rows(rows):
    values = rows.astype(F32)
    return (values * lax.rsqrt(jnp.sum(values * values, axis=1, keepdims=True) + EPS)).astype(BF)


def placed(rows, target, start, count):
    places = lax.broadcasted_iota(jnp.int32, (count, target.shape[1]), 0) + start
    pick = jnp.where(places == target, 1.0, 0.0).astype(BF)
    return dot(pick, rows).astype(BF)


def giant_pack_kernel(
    embed_hbm, assign_hbm, slot_hbm, giant_ref, lines_ref, embed_ref, assign_ref, slot_ref, sems
):
    parts = (pl.ds(0, LANES), pl.ds(LANES, embed_ref.shape[0] - LANES))
    copies = [
        pltpu.make_async_copy(assign_hbm, assign_ref, sems.at[0]),
        pltpu.make_async_copy(slot_hbm, slot_ref, sems.at[1]),
    ]
    copies += [
        pltpu.make_async_copy(embed_hbm.at[part], embed_ref.at[part], sems.at[2 + number])
        for number, part in enumerate(parts)
    ]
    for copy in copies:
        copy.start()
    copies[0].wait()
    copies[1].wait()
    assign = assign_ref[...].reshape(1, -1)
    lines_ref[...] = assign
    target = (slot_ref[...].reshape(1, -1) & 1) * GROUP + assign - OWNERS
    target = jnp.where(assign >= OWNERS, target, -1)
    places = lax.broadcasted_iota(jnp.int32, (2 * GROUP, target.shape[1]), 0)
    pick = jnp.where(places == target, 1.0, 0.0).astype(BF)
    copies[2].wait()
    rows = dot(pick[:, :LANES], embed_ref[:LANES])
    copies[3].wait()
    rows = (rows + dot(pick[:, LANES:], embed_ref[LANES:])).astype(BF)
    for number in range(2):
        part = rows[number * GROUP : (number + 1) * GROUP]
        giant_ref[:, number] = part.reshape(GROUP, SUB, LANES)


def giant_pack(embed, assign, slot):
    return pl.pallas_call(
        giant_pack_kernel,
        in_specs=[pl.BlockSpec(memory_space=pl.ANY)] * 3,
        out_shape=[
            jax.ShapeDtypeStruct((GROUP, 2, SUB, LANES), BF),
            jax.ShapeDtypeStruct((1, assign.shape[0]), jnp.int32),
        ],
        scratch_shapes=[
            pltpu.VMEM(embed.shape, BF),
            pltpu.VMEM(assign.shape, jnp.int32),
            pltpu.VMEM(slot.shape, jnp.int32),
            pltpu.SemaphoreType.DMA((4,)),
        ],
        compiler_params=params(56),
        name="giant_pack",
    )(embed, assign, slot)


def pack_kernel(embed_ref, assign_ref, same_ref, *other_refs):
    core = lax.axis_index("core")
    assign = assign_ref[...]
    chip = (assign // (2 * RUN)) * RUN + (assign & (RUN - 1))
    other = ((assign // RUN) & 1) != core
    target = jnp.where(assign >= OWNERS, -1, jnp.where(other, CHIPS, 0) + chip)
    unit = unit_rows(embed_ref[...])
    half = CHIPS // 2
    for number, ref in enumerate(other_refs):
        rows = placed(unit, target, CHIPS + number * half, half)
        ref[...] = rows.reshape(half, SUB, LANES)
    for start in (0, half):
        rows = placed(unit, target, start, half)
        same_ref[start : start + half] = rows.reshape(half, SUB, LANES)


def pack(embed, assign):
    shape = lambda rows: jax.ShapeDtypeStruct((rows, SUB, LANES), BF)
    return pl.pallas_call(
        pack_kernel,
        out_shape=[shape(CHIPS), shape(CHIPS // 2), shape(CHIPS // 2)],
        compiler_params=params(),
        name="pack",
    )(embed, assign)


def join_kernel(same_ref, low_ref, high_ref, both_ref, sems):
    core = lax.axis_index("core")
    half = CHIPS // 2
    copies = [
        pltpu.make_async_copy(same_ref, both_ref.at[:, core], sems.at[0]),
        pltpu.make_async_copy(low_ref, both_ref.at[pl.ds(0, half), 1 - core], sems.at[1]),
        pltpu.make_async_copy(high_ref, both_ref.at[pl.ds(half, half), 1 - core], sems.at[2]),
    ]
    for copy in copies:
        copy.start()
    for copy in copies:
        copy.wait()


def join(*parts):
    return pl.pallas_call(
        join_kernel,
        in_specs=[pl.BlockSpec(memory_space=pl.ANY)] * 3,
        out_specs=pl.BlockSpec(memory_space=pl.ANY),
        out_shape=jax.ShapeDtypeStruct((CHIPS, 2, SUB, LANES), BF),
        scratch_shapes=[pltpu.SemaphoreType.DMA((3,))],
        compiler_params=params(),
        cost_estimate=pl.CostEstimate(flops=0, bytes_accessed=0, transcendentals=0),
        name="join",
    )(*parts)


def gate_kernel(*_):
    pass


def gate(tiles, ready):
    anywhere = pl.BlockSpec(memory_space=pl.ANY)
    return pl.pallas_call(
        gate_kernel,
        in_specs=[anywhere, anywhere],
        out_specs=anywhere,
        out_shape=jax.ShapeDtypeStruct(tiles.shape, BF),
        input_output_aliases={0: 0},
        compiler_params=params(),
        name="gate",
    )(tiles, ready)


def block(ref):
    return ref[...].reshape(2 * GROUP, WIDTH)


def eye(size):
    return lax.broadcasted_iota(jnp.int32, (size, size), 0) == lax.broadcasted_iota(
        jnp.int32, (size, size), 1
    )


def live_of(rows):
    products = dot_t(rows, rows)
    down, across = [], []
    for start in range(0, rows.shape[0], LANES):
        part = products[start : start + LANES, start : start + LANES]
        diagonal = jnp.where(eye(LANES), part, NONE)
        down.append(jnp.max(diagonal, axis=1, keepdims=True) > 0.25)
        across.append(jnp.max(diagonal, axis=0, keepdims=True) > 0.25)
    return products, down, jnp.concatenate(across, axis=1)


def top(products, down, own=None):
    best = None
    for number, live in enumerate(down):
        part = products[number * LANES : (number + 1) * LANES]
        part = jnp.where(live & ~eye(LANES) if number == own else live, part, NONE)
        part = jnp.max(part, axis=0, keepdims=True)
        best = part if best is None else jnp.maximum(best, part)
    return best


def column_sum(products, down):
    total = None
    for number, live in enumerate(down):
        part = jnp.where(live, products[number * LANES : (number + 1) * LANES], 0.0)
        part = jnp.sum(part, axis=0, keepdims=True)
        total = part if total is None else total + part
    return total


def block_sum(rows, across):
    mask = jnp.broadcast_to(jnp.where(across, 1.0, 0.0), (8, rows.shape[0])).astype(BF)
    return dot(mask, rows)[0:1]


def first_kernel(mine_ref, near_ref, far_ref, rows_ref, unit_ref):
    rows_ref[0] = unit_rows(block(mine_ref))
    rows_ref[1] = unit_rows(block(near_ref))
    far = unit_rows(block(far_ref))
    rows_ref[2] = far
    unit_ref[...] = far.reshape(unit_ref.shape)


def unit_blocks(mine, near, far):
    return pl.pallas_call(
        first_kernel,
        out_shape=[
            jax.ShapeDtypeStruct((3, 2 * GROUP, WIDTH), BF),
            jax.ShapeDtypeStruct(far.shape, BF),
        ],
        compiler_params=params(),
        name="unit_blocks",
    )(mine, near, far)


def pairs_kernel(rows_ref, best_ref, sums_ref, one_ref, two_ref):
    mine, near, far = rows_ref[0], rows_ref[1], rows_ref[2]
    squares, mine_down, mine_across = live_of(mine)
    _, near_down, near_across = live_of(near)
    _, far_down, far_across = live_of(far)
    best = top(squares, mine_down, 0)
    best = jnp.maximum(best, top(dot_t(near, mine), near_down))
    best_ref[0:1] = jnp.maximum(best, top(dot_t(far, mine), far_down))
    best_ref[1:2] = jnp.where(mine_across, 1.0, 0.0)
    best_near = jnp.maximum(top(dot_t(mine, near), mine_down), top(dot_t(far, near), far_down))
    best_far = jnp.maximum(top(dot_t(mine, far), mine_down), top(dot_t(near, far), near_down))
    sum_mine = block_sum(mine, mine_across)
    sum_near = block_sum(near, near_across)
    sum_far = block_sum(far, far_across)
    sums_ref[0:1] = sum_mine
    sums_ref[1:2] = sum_near
    sums_ref[2:3] = sum_far
    one_ref[0:1] = sum_mine
    one_ref[1:2] = sum_far
    one_ref[2:3] = jnp.concatenate([best_near] * SUB, axis=1)
    two_ref[0:1] = sum_mine
    two_ref[1:2] = sum_near
    two_ref[2:3] = jnp.concatenate([best_far] * SUB, axis=1)


def pairs(rows):
    message = jax.ShapeDtypeStruct((3, WIDTH), F32)
    return pl.pallas_call(
        pairs_kernel,
        out_shape=[jax.ShapeDtypeStruct((2, 2 * GROUP), F32), message, message, message],
        compiler_params=params(),
        cost_estimate=LONG,
        name="pairs",
    )(rows)


def scale_of(total):
    return lax.rsqrt(jnp.sum(total * total) + EPS)


def products_with(total, rows):
    high, mid, low = three(total)
    parts = jnp.concatenate([high, mid, low, jnp.zeros((5, WIDTH), BF)], axis=0)
    found = dot_t(parts, rows)
    return found[0:1] + found[1:2] + found[2:3]


def early_kernel(rows_ref, best_ref, sums_ref, one_ref, two_ref, some_ref, held_ref):
    sign, col = sign_and_col()
    best = best_ref[0:1]
    for ref in (one_ref, two_ref):
        best = jnp.maximum(best, ref[2:3, : 2 * GROUP])
    held_ref[...] = jnp.zeros_like(held_ref)
    total = jnp.zeros((1, WIDTH), F32)
    for offset, row in (
        (0, sums_ref[0:1]),
        (1, sums_ref[1:2]),
        (6, sums_ref[2:3]),
        (7, one_ref[0:1]),
        (5, one_ref[1:2]),
        (2, two_ref[0:1]),
        (3, two_ref[1:2]),
    ):
        held_ref[pl.ds((col + sign * offset) & (N_COL - 1), 1)] = row
        total = total + row
    some_ref[0:1] = best
    some_ref[1:2] = products_with(total, rows_ref[0])
    some_ref[2:3] = best_ref[1:2]


def early(*operands):
    return pl.pallas_call(
        early_kernel,
        out_shape=[
            jax.ShapeDtypeStruct((3, 2 * GROUP), F32),
            jax.ShapeDtypeStruct((N_COL, WIDTH), F32),
        ],
        compiler_params=params(),
        name="early",
    )(*operands)


def giant_kernel(rows_ref, some_ref, held_ref, last_ref, max_ref, cos_ref, center_ref):
    sign, col = sign_and_col()
    last = block(last_ref)
    _, down, across = live_of(last)
    products = dot_t(last, rows_ref[0])
    place = (col + sign * 4) & (N_COL - 1)
    held = held_ref[...]
    is_last = lax.broadcasted_iota(jnp.int32, held.shape, 0) == place
    held = jnp.where(is_last, block_sum(last, across), held)
    total = held[0:1]
    for number in range(1, N_COL):
        total = total + held[number : number + 1]
    scale = scale_of(total)
    live = some_ref[2:3] > 0.0
    max_ref[...] = jnp.where(live, jnp.maximum(some_ref[0:1], top(products, down)), 0.0)
    cos_ref[...] = jnp.where(live, (some_ref[1:2] + column_sum(products, down)) * scale, 0.0)
    center_ref[...] = total * scale


def normal_kernel(tiles_ref, max_ref, cos_ref, center_ref, rows_ref):
    for y in range(CHIPS // RUN):
        for core in range(2):
            start = (2 * y + core) * RUN
            rows_ref[start : start + RUN] = tiles_ref[y * RUN : (y + 1) * RUN, core].reshape(
                RUN, WIDTH
            )
    rows = rows_ref[...]
    products, down, across = live_of(rows)
    total = block_sum(rows, across)
    scale = scale_of(total)
    center_ref[...] = total * scale
    best = [
        top(products[:, number * LANES : (number + 1) * LANES], down, number)
        for number in range(len(down))
    ]
    max_ref[...] = jnp.where(across, jnp.concatenate(best, axis=1), 0.0)
    cos_ref[...] = jnp.where(across, column_sum(products, down) * scale, 0.0)


def tail_kernel(tiles_ref, rows_ref, some_ref, held_ref, last_ref, *refs):
    *outs, scratch_ref = refs
    giant_kernel(rows_ref, some_ref, held_ref, last_ref, *outs[3:])
    normal_kernel(tiles_ref, *outs[:3], scratch_ref)


def tail(*operands):
    row = lambda size: jax.ShapeDtypeStruct((1, size), F32)
    return pl.pallas_call(
        tail_kernel,
        out_shape=[row(OWNERS), row(OWNERS), row(WIDTH), row(2 * GROUP), row(2 * GROUP), row(WIDTH)],
        scratch_shapes=[pltpu.VMEM((OWNERS, WIDTH), BF)],
        compiler_params=params(),
        name="tail",
    )(*operands)


def along(rows, offset):
    moves = []
    for src in range(N_SRC):
        for col in range(N_COL):
            goal = (col + (offset if src % 2 == 0 else -offset)) % N_COL
            moves.append((src * N_COL + col, src * N_COL + goal))
    return lax.ppermute(rows, ("y", "core", "col"), moves)


def to_other_core(rows):
    return lax.ppermute(rows, "core", [(0, 1), (1, 0)])


def all_to_all(rows, axes):
    return lax.all_to_all(rows, axes, split_axis=0, concat_axis=0, tiled=True)


def per_device(embed, assign, slot):
    giant, lines = giant_pack(embed, assign, slot)
    giant = all_to_all(giant, ("y", "core", "clu"))
    same, low, high = pack(embed, lines)
    both = join(same, to_other_core(low), to_other_core(high))
    mine = gate(giant, both)
    near, far = along(mine, 7), along(mine, 2)
    both = all_to_all(both, ("y", "clu", "col"))
    rows, far = unit_blocks(mine, near, far)
    last = along(far, 2)
    best, sums, one, two = pairs(rows)
    one, two = along(one, 1), along(two, 6)
    some, held = early(rows, best, sums, one, two)
    return tuple(tail(both, rows, some, held, last))


def solution(mesh):
    fine = Mesh(mesh.devices.reshape(N_SRC // 2, 2, -1, N_COL), ("y", "core", "clu", "col"))
    plane = ("y", "core", "clu")
    everywhere = (*plane, "col")
    in_specs = (P(everywhere, None), P(everywhere), P(everywhere))
    out_specs = (
        P(everywhere, None),
        P(everywhere, None),
        P(everywhere, None),
        P(plane, "col"),
        P(plane, "col"),
        P(plane, None),
    )
    return jax.shard_map(
        per_device, mesh=fine, in_specs=in_specs, out_specs=out_specs, check_vma=False
    )
```

```python
import jax
import jax.numpy as jnp
from jax import lax
from jax.experimental import pallas as pl
from jax.experimental.pallas import tpu as pltpu
from jax.sharding import Mesh
from jax.sharding import PartitionSpec as P

N_COL = 8
N_SRC = 16
GROUP = 64
OWNERS = GROUP * N_COL
CHIPS = OWNERS // 2
RUN = 32
WIDTH = 1024
LANES = 128
SUB = WIDTH // LANES
EPS = 1e-06
NONE = -4.0

BF = jnp.bfloat16
F32 = jnp.float32


LONG = pl.CostEstimate(flops=30_000_000_000, bytes_accessed=2_000_000, transcendentals=0)


def params(mib=12):
    return pltpu.CompilerParams(vmem_limit_bytes=mib * 1024 * 1024)


def dot_t(left, right):
    return lax.dot_general(left, right, (((1,), (1,)), ((), ())), preferred_element_type=F32)


def dot(left, right):
    return jnp.dot(left, right, preferred_element_type=F32)


def three(values):
    high = values.astype(BF)
    rest = values - high.astype(F32)
    mid = rest.astype(BF)
    low = (rest - mid.astype(F32)).astype(BF)
    return high, mid, low


def sign_and_col():
    return 1 - 2 * lax.axis_index("core"), lax.axis_index("col")


def unit_rows(rows):
    values = rows.astype(F32)
    return (values * lax.rsqrt(jnp.sum(values * values, axis=1, keepdims=True) + EPS)).astype(BF)


def placed(rows, target, start, count):
    places = lax.broadcasted_iota(jnp.int32, (count, target.shape[1]), 0) + start
    pick = jnp.where(places == target, 1.0, 0.0).astype(BF)
    return dot(pick, rows).astype(BF)


def giant_pack_kernel(
    embed_hbm, assign_hbm, slot_hbm, giant_ref, embed_ref, assign_ref, slot_ref, sems
):
    parts = (pl.ds(0, LANES), pl.ds(LANES, embed_ref.shape[0] - LANES))
    copies = [
        pltpu.make_async_copy(assign_hbm, assign_ref, sems.at[0]),
        pltpu.make_async_copy(slot_hbm, slot_ref, sems.at[1]),
    ]
    copies += [
        pltpu.make_async_copy(embed_hbm.at[part], embed_ref.at[part], sems.at[2 + number])
        for number, part in enumerate(parts)
    ]
    for copy in copies:
        copy.start()
    copies[0].wait()
    copies[1].wait()
    assign = assign_ref[...].reshape(1, -1)
    target = (slot_ref[...].reshape(1, -1) & 1) * GROUP + assign - OWNERS
    target = jnp.where(assign >= OWNERS, target, -1)
    places = lax.broadcasted_iota(jnp.int32, (2 * GROUP, target.shape[1]), 0)
    pick = jnp.where(places == target, 1.0, 0.0).astype(BF)
    copies[2].wait()
    rows = dot(pick[:, :LANES], embed_ref[:LANES])
    copies[3].wait()
    rows = (rows + dot(pick[:, LANES:], embed_ref[LANES:])).astype(BF)
    for number in range(2):
        part = rows[number * GROUP : (number + 1) * GROUP]
        giant_ref[:, number] = part.reshape(GROUP, SUB, LANES)


def giant_pack(embed, assign, slot):
    return pl.pallas_call(
        giant_pack_kernel,
        in_specs=[pl.BlockSpec(memory_space=pl.ANY)] * 3,
        out_shape=jax.ShapeDtypeStruct((GROUP, 2, SUB, LANES), BF),
        scratch_shapes=[
            pltpu.VMEM(embed.shape, BF),
            pltpu.VMEM(assign.shape, jnp.int32),
            pltpu.VMEM(slot.shape, jnp.int32),
            pltpu.SemaphoreType.DMA((4,)),
        ],
        compiler_params=params(56),
        name="giant_pack",
    )(embed, assign, slot)


def pack_kernel(embed_ref, assign_ref, same_ref, *other_refs):
    core = lax.axis_index("core")
    assign = assign_ref[...].reshape(1, -1)
    chip = (assign // (2 * RUN)) * RUN + (assign & (RUN - 1))
    other = ((assign // RUN) & 1) != core
    target = jnp.where(assign >= OWNERS, -1, jnp.where(other, CHIPS, 0) + chip)
    unit = unit_rows(embed_ref[...])
    half = CHIPS // 2
    for number, ref in enumerate(other_refs):
        rows = placed(unit, target, CHIPS + number * half, half)
        ref[...] = rows.reshape(half, SUB, LANES)
    for start in (0, half):
        rows = placed(unit, target, start, half)
        same_ref[start : start + half] = rows.reshape(half, SUB, LANES)


def pack(embed, assign):
    shape = lambda rows: jax.ShapeDtypeStruct((rows, SUB, LANES), BF)
    return pl.pallas_call(
        pack_kernel,
        out_shape=[shape(CHIPS), shape(CHIPS // 2), shape(CHIPS // 2)],
        compiler_params=params(),
        name="pack",
    )(embed, assign)


def join_kernel(same_ref, low_ref, high_ref, both_ref, sems):
    core = lax.axis_index("core")
    half = CHIPS // 2
    copies = [
        pltpu.make_async_copy(same_ref, both_ref.at[:, core], sems.at[0]),
        pltpu.make_async_copy(low_ref, both_ref.at[pl.ds(0, half), 1 - core], sems.at[1]),
        pltpu.make_async_copy(high_ref, both_ref.at[pl.ds(half, half), 1 - core], sems.at[2]),
    ]
    for copy in copies:
        copy.start()
    for copy in copies:
        copy.wait()


def join(*parts):
    return pl.pallas_call(
        join_kernel,
        in_specs=[pl.BlockSpec(memory_space=pl.ANY)] * 3,
        out_specs=pl.BlockSpec(memory_space=pl.ANY),
        out_shape=jax.ShapeDtypeStruct((CHIPS, 2, SUB, LANES), BF),
        scratch_shapes=[pltpu.SemaphoreType.DMA((3,))],
        compiler_params=params(),
        cost_estimate=pl.CostEstimate(flops=0, bytes_accessed=0, transcendentals=0),
        name="join",
    )(*parts)


def gate_kernel(tiles_ref, _, out_ref):
    out_ref[...] = tiles_ref[...]


def gate(tiles, ready):
    return pl.pallas_call(
        gate_kernel,
        in_specs=[pl.BlockSpec(memory_space=pltpu.VMEM), pl.BlockSpec(memory_space=pl.ANY)],
        out_shape=jax.ShapeDtypeStruct(tiles.shape, BF),
        compiler_params=params(),
        name="gate",
    )(tiles, ready)


def block(ref):
    return ref[...].reshape(2 * GROUP, WIDTH)


def eye(size):
    return lax.broadcasted_iota(jnp.int32, (size, size), 0) == lax.broadcasted_iota(
        jnp.int32, (size, size), 1
    )


def live_of(rows):
    products = dot_t(rows, rows)
    down, across = [], []
    for start in range(0, rows.shape[0], LANES):
        part = products[start : start + LANES, start : start + LANES]
        diagonal = jnp.where(eye(LANES), part, NONE)
        down.append(jnp.max(diagonal, axis=1, keepdims=True) > 0.25)
        across.append(jnp.max(diagonal, axis=0, keepdims=True) > 0.25)
    return products, down, jnp.concatenate(across, axis=1)


def top(products, down, own=None):
    best = None
    for number, live in enumerate(down):
        part = products[number * LANES : (number + 1) * LANES]
        part = jnp.where(live & ~eye(LANES) if number == own else live, part, NONE)
        part = jnp.max(part, axis=0, keepdims=True)
        best = part if best is None else jnp.maximum(best, part)
    return best


def column_sum(products, down):
    total = None
    for number, live in enumerate(down):
        part = jnp.where(live, products[number * LANES : (number + 1) * LANES], 0.0)
        part = jnp.sum(part, axis=0, keepdims=True)
        total = part if total is None else total + part
    return total


def block_sum(rows, across):
    mask = jnp.broadcast_to(jnp.where(across, 1.0, 0.0), (8, rows.shape[0])).astype(BF)
    return dot(mask, rows)[0:1]


def first_kernel(mine_ref, near_ref, far_ref, rows_ref, unit_ref):
    rows_ref[0] = unit_rows(block(mine_ref))
    rows_ref[1] = unit_rows(block(near_ref))
    far = unit_rows(block(far_ref))
    rows_ref[2] = far
    unit_ref[...] = far.reshape(unit_ref.shape)


def unit_blocks(mine, near, far):
    return pl.pallas_call(
        first_kernel,
        out_shape=[
            jax.ShapeDtypeStruct((3, 2 * GROUP, WIDTH), BF),
            jax.ShapeDtypeStruct(far.shape, BF),
        ],
        compiler_params=params(),
        name="unit_blocks",
    )(mine, near, far)


def pairs_kernel(rows_ref, best_ref, sums_ref, one_ref, two_ref):
    mine, near, far = rows_ref[0], rows_ref[1], rows_ref[2]
    squares, mine_down, mine_across = live_of(mine)
    _, near_down, near_across = live_of(near)
    _, far_down, far_across = live_of(far)
    best = top(squares, mine_down, 0)
    best = jnp.maximum(best, top(dot_t(near, mine), near_down))
    best_ref[0:1] = jnp.maximum(best, top(dot_t(far, mine), far_down))
    best_ref[1:2] = jnp.where(mine_across, 1.0, 0.0)
    best_near = jnp.maximum(top(dot_t(mine, near), mine_down), top(dot_t(far, near), far_down))
    best_far = jnp.maximum(top(dot_t(mine, far), mine_down), top(dot_t(near, far), near_down))
    sum_mine = block_sum(mine, mine_across)
    sum_near = block_sum(near, near_across)
    sum_far = block_sum(far, far_across)
    sums_ref[0:1] = sum_mine
    sums_ref[1:2] = sum_near
    sums_ref[2:3] = sum_far
    one_ref[0:1] = sum_mine
    one_ref[1:2] = sum_far
    one_ref[2:3] = jnp.concatenate([best_near] * SUB, axis=1)
    two_ref[0:1] = sum_mine
    two_ref[1:2] = sum_near
    two_ref[2:3] = jnp.concatenate([best_far] * SUB, axis=1)


def pairs(rows):
    message = jax.ShapeDtypeStruct((3, WIDTH), F32)
    return pl.pallas_call(
        pairs_kernel,
        out_shape=[jax.ShapeDtypeStruct((2, 2 * GROUP), F32), message, message, message],
        compiler_params=params(),
        cost_estimate=LONG,
        name="pairs",
    )(rows)


def scale_of(total):
    return lax.rsqrt(jnp.sum(total * total) + EPS)


def products_with(total, rows):
    high, mid, low = three(total)
    parts = jnp.concatenate([high, mid, low, jnp.zeros((5, WIDTH), BF)], axis=0)
    found = dot_t(parts, rows)
    return found[0:1] + found[1:2] + found[2:3]


def early_kernel(rows_ref, best_ref, sums_ref, one_ref, two_ref, some_ref, held_ref):
    sign, col = sign_and_col()
    best = best_ref[0:1]
    for ref in (one_ref, two_ref):
        best = jnp.maximum(best, ref[2:3, : 2 * GROUP])
    held_ref[...] = jnp.zeros_like(held_ref)
    total = jnp.zeros((1, WIDTH), F32)
    for offset, row in (
        (0, sums_ref[0:1]),
        (1, sums_ref[1:2]),
        (6, sums_ref[2:3]),
        (7, one_ref[0:1]),
        (5, one_ref[1:2]),
        (2, two_ref[0:1]),
        (3, two_ref[1:2]),
    ):
        held_ref[pl.ds((col + sign * offset) & (N_COL - 1), 1)] = row
        total = total + row
    some_ref[0:1] = best
    some_ref[1:2] = products_with(total, rows_ref[0])
    some_ref[2:3] = best_ref[1:2]


def early(*operands):
    return pl.pallas_call(
        early_kernel,
        out_shape=[
            jax.ShapeDtypeStruct((3, 2 * GROUP), F32),
            jax.ShapeDtypeStruct((N_COL, WIDTH), F32),
        ],
        compiler_params=params(),
        name="early",
    )(*operands)


def giant_kernel(rows_ref, some_ref, held_ref, last_ref, max_ref, cos_ref, center_ref):
    sign, col = sign_and_col()
    last = block(last_ref)
    _, down, across = live_of(last)
    products = dot_t(last, rows_ref[0])
    place = (col + sign * 4) & (N_COL - 1)
    held = held_ref[...]
    is_last = lax.broadcasted_iota(jnp.int32, held.shape, 0) == place
    held = jnp.where(is_last, block_sum(last, across), held)
    total = held[0:1]
    for number in range(1, N_COL):
        total = total + held[number : number + 1]
    scale = scale_of(total)
    live = some_ref[2:3] > 0.0
    max_ref[...] = jnp.where(live, jnp.maximum(some_ref[0:1], top(products, down)), 0.0)
    cos_ref[...] = jnp.where(live, (some_ref[1:2] + column_sum(products, down)) * scale, 0.0)
    center_ref[...] = total * scale


def normal_kernel(tiles_ref, max_ref, cos_ref, center_ref, rows_ref):
    for y in range(CHIPS // RUN):
        for core in range(2):
            start = (2 * y + core) * RUN
            rows_ref[start : start + RUN] = tiles_ref[y * RUN : (y + 1) * RUN, core].reshape(
                RUN, WIDTH
            )
    rows = rows_ref[...]
    products, down, across = live_of(rows)
    total = block_sum(rows, across)
    scale = scale_of(total)
    center_ref[...] = total * scale
    best = [
        top(products[:, number * LANES : (number + 1) * LANES], down, number)
        for number in range(len(down))
    ]
    max_ref[...] = jnp.where(across, jnp.concatenate(best, axis=1), 0.0)
    cos_ref[...] = jnp.where(across, column_sum(products, down) * scale, 0.0)


def tail_kernel(tiles_ref, rows_ref, some_ref, held_ref, last_ref, *refs):
    *outs, scratch_ref = refs
    giant_kernel(rows_ref, some_ref, held_ref, last_ref, *outs[3:])
    normal_kernel(tiles_ref, *outs[:3], scratch_ref)


def tail(*operands):
    row = lambda size: jax.ShapeDtypeStruct((1, size), F32)
    return pl.pallas_call(
        tail_kernel,
        out_shape=[row(OWNERS), row(OWNERS), row(WIDTH), row(2 * GROUP), row(2 * GROUP), row(WIDTH)],
        scratch_shapes=[pltpu.VMEM((OWNERS, WIDTH), BF)],
        compiler_params=params(),
        name="tail",
    )(*operands)


def along(rows, offset):
    moves = []
    for src in range(N_SRC):
        for col in range(N_COL):
            goal = (col + (offset if src % 2 == 0 else -offset)) % N_COL
            moves.append((src * N_COL + col, src * N_COL + goal))
    return lax.ppermute(rows, ("y", "core", "col"), moves)


def to_other_core(rows):
    return lax.ppermute(rows, "core", [(0, 1), (1, 0)])


def all_to_all(rows, axes):
    return lax.all_to_all(rows, axes, split_axis=0, concat_axis=0, tiled=True)


def per_device(embed, assign, slot):
    giant = giant_pack(embed, assign, slot)
    giant = all_to_all(giant, ("y", "core", "clu"))
    same, low, high = pack(embed, assign)
    both = join(same, to_other_core(low), to_other_core(high))
    mine = gate(giant, both)
    near, far = along(mine, 7), along(mine, 2)
    both = all_to_all(both, ("y", "clu", "col"))
    rows, far = unit_blocks(mine, near, far)
    last = along(far, 2)
    best, sums, one, two = pairs(rows)
    one, two = along(one, 1), along(two, 6)
    some, held = early(rows, best, sums, one, two)
    return tuple(tail(both, rows, some, held, last))


def solution(mesh):
    fine = Mesh(mesh.devices.reshape(N_SRC // 2, 2, -1, N_COL), ("y", "core", "clu", "col"))
    plane = ("y", "core", "clu")
    everywhere = (*plane, "col")
    in_specs = (P(everywhere, None), P(everywhere), P(everywhere))
    out_specs = (
        P(everywhere, None),
        P(everywhere, None),
        P(everywhere, None),
        P(plane, "col"),
        P(plane, "col"),
        P(plane, None),
    )
    return jax.shard_map(
        per_device, mesh=fine, in_specs=in_specs, out_specs=out_specs, check_vma=False
    )
```
